32 devices in a mesh: groups: 2 (over x), attn: 16 (over z, y, core).
Axes of the slice: x: 2, y: 2, z: 4, core: 2. Of those that a mesh axis runs over, the one named last changes fastest.
Arguments:
- queries: bfloat16 [384, 6144], P(('groups', 'attn')), parts along dimension 0, may hold values from -64 to 64
- residual: bfloat16 [384, 6144], P(('groups', 'attn')), parts along dimension 0, may hold values from -6 to 6
- new_keys: bfloat16 [384, 1024], P(('groups', 'attn')), parts along dimension 0, may hold values from -6 to 6
- new_values: bfloat16 [384, 1024], P(('groups', 'attn')), parts along dimension 0, may hold values from -6 to 6
- key_pool: bfloat16 [3072, 16, 1024], P(('groups', 'attn')), parts along dimension 0, may hold values from -4 to 4
- value_pool: bfloat16 [3072, 16, 1024], P(('groups', 'attn')), parts along dimension 0, may hold values from -6 to 6
- page_table: int32 [384, 8], P(('groups', 'attn')), parts along dimension 0, may hold values from 0 to 95, as said below
- lengths: int32 [384], P(('groups', 'attn')), parts along dimension 0, may hold values from 2 to 127
- migrate: int32 [64], P(('groups', 'attn')), parts along dimension 0, may hold values from 0 to 11, as said below
- chosen: int32 [384, 2], P(('groups', 'attn')), parts along dimension 0, may hold values from 0 to 7, as said below
- router_weight: bfloat16 [6144, 8], replicated, may hold values from -0.078125 to 0.078125
- w_gate: bfloat16 [6144, 2048], P(None, 'attn'), may hold values from -0.078125 to 0.078125
- w_up: bfloat16 [6144, 2048], P(None, 'attn'), may hold values from -0.078125 to 0.078125
- w_down: bfloat16 [2048, 6144], P('attn'), may hold values from -0.1875 to 0.1875
Outputs:
- mixed: bfloat16 [384, 6144], P(('groups', 'attn')), parts along dimension 0
- moved_keys: bfloat16 [64, 128, 1024], P(('groups', 'attn')), parts along dimension 0
- moved_values: bfloat16 [64, 128, 1024], P(('groups', 'attn')), parts along dimension 0
The draws below stay inside these ranges and needn't reach their ends.
There are 2 independent parts, one for each index of `groups`. The reference program is written for one: setup_inputs(seed, part) draws one part's arguments, and reference() takes and returns one part's arrays. A program takes and returns all parts, laid end to end along the dimension named above; an argument that names none is the same for every part. Nothing has to cross between parts.
Inputs may be any that keep to these rules, and one draw needn't show every extreme that they name: `page_table`: the 8 entries of the 12 requests of one device name every page 0 to 95 of that device once. `migrate`: the 2 entries of one device are different slots of its requests. `chosen`: A request names two different experts. Of the requests of one device at most 5 name expert e, for each e < 2, and for each such e some device has exactly 5.
All inputs are finite; a program needn't handle non-finite values.
Results may differ from the reference program's by a relative error of at most 0.0065.
Values may be sent and summed in bfloat16 or wider, within the bound.
No kernel may reach another device: no remote copies, remote signals or barrier semaphores. Data moves between devices by JAX's collectives and lax.ppermute only.
A program may use at most 192 MiB of HBM per device.

```python
import math
import jax
import jax.numpy as jnp
from jax import lax

D = 6144
HEADS = 48
KV_HEADS = 8
HEAD_DIM = 128
EXPERTS = 8
REQ_DEV = 12
CAP = 5
MIGC = 2
MAXP = 8
PAGE = 16
EXP_ON = 2
KVD = 1024
S = 128
PAGES_DEV = 96
ROWS = 192
MOVED = 32
FFW = 1024
N_ATTN = 16


def page_layout(base_key):
    table_key = jax.random.fold_in(base_key, 101)
    device_keys = jax.random.split(table_key, ROWS // REQ_DEV)

    def one_device(device_key):
        return jax.random.permutation(device_key, PAGES_DEV).reshape(REQ_DEV, MAXP)
    return jax.vmap(one_device)(device_keys).reshape(ROWS, MAXP).astype(jnp.int32)


def draw_page_table(key, part):
    return page_layout(key)


def draw_key_pool(key, part):
    folded = jax.random.fold_in(key, 3)
    values = jnp.clip(jax.random.normal(folded, (ROWS // REQ_DEV * PAGES_DEV, PAGE, KV_HEADS * HEAD_DIM), jnp.float32), -4.0, 4.0)
    return values.astype(jnp.bfloat16)


def draw_queries(key, part):
    folded = jax.random.fold_in(key, 5)
    row_shape = (ROWS, HEADS * HEAD_DIM)
    values = jnp.clip(jax.random.normal(folded, row_shape, jnp.float32), -6.0, 6.0)
    return values.astype(jnp.bfloat16)


def draw_migrate(key, part):
    folded = jax.random.fold_in(key, 7)
    device_keys = jax.random.split(folded, ROWS // REQ_DEV)

    def one_device(device_key):
        return jax.random.permutation(device_key, REQ_DEV)[:MIGC]
    return jax.vmap(one_device)(device_keys).reshape(-1).astype(jnp.int32)


def draw_chosen(key, part):
    folded = jax.random.fold_in(key, 9)
    device_total = ROWS // REQ_DEV
    split_keys = jax.random.split(folded, 6)
    per_device = jax.random.randint(split_keys[0], (device_total, EXP_ON), 1, CAP + 1)
    busiest = jax.random.randint(split_keys[1], (EXP_ON,), 0, device_total)
    device_ids = jnp.arange(device_total, dtype=jnp.int32)[:, None]
    per_device = jnp.where(device_ids == busiest[None, :], CAP, per_device)
    order_keys = jax.random.split(split_keys[2], device_total * EXP_ON)

    def rank_of(order_key):
        shuffled = jax.random.permutation(order_key, REQ_DEV)
        return jnp.zeros((REQ_DEV,), jnp.int32).at[shuffled].set(jnp.arange(REQ_DEV, dtype=jnp.int32))
    ranks = jax.vmap(rank_of)(order_keys).reshape(device_total, EXP_ON, REQ_DEV)
    wanted = ranks < per_device[:, :, None]
    first_use = wanted[:, 0].reshape(ROWS)
    second_use = wanted[:, 1].reshape(ROWS)
    others = EXPERTS - EXP_ON
    other_first = jax.random.randint(split_keys[3], (ROWS,), 0, others) + EXP_ON
    offset_draw = jax.random.randint(split_keys[4], (ROWS,), 1, others)
    other_second = EXP_ON + (other_first - EXP_ON + offset_draw) % others
    leading = jnp.where(first_use, 0, jnp.where(second_use, 1, other_first))
    trailing = jnp.where(first_use & second_use, 1, jnp.where(first_use | second_use, other_first, other_second))
    flipped = jax.random.randint(split_keys[5], (ROWS,), 0, 2) == 1
    column_first = jnp.where(flipped, trailing, leading)
    column_second = jnp.where(flipped, leading, trailing)
    return jnp.stack([column_first, column_second], axis=1).astype(jnp.int32)


def with_ends(values, own_key, low, largest):
    place = [jax.random.randint(jax.random.fold_in(own_key, axis), (), 0, length) for axis, length in enumerate(values.shape)]
    longest = values.shape.index(max(values.shape))
    neighbour = place[:longest] + [(place[longest] + 1) % values.shape[longest]] + place[longest + 1:]
    return values.at[tuple(place)].set(low).at[tuple(neighbour)].set(largest)


def block_levels(key, dims, shards, low, top_value):
    gain = 1.0
    for dim, parts in shards:
        heights = jax.random.uniform(jax.random.fold_in(jax.random.fold_in(key, 6), dim), (parts,), jnp.float32, low / len(shards), top_value / len(shards))
        gain = gain * jnp.repeat(jnp.exp(heights), dims[dim] // parts).reshape((-1,) + (1,) * (len(dims) - 1 - dim))
    return gain


def normal_values(stream_key, shape, width, reach, cuts=(), held_as=jnp.bfloat16):
    drawn = jax.random.normal(stream_key, shape, jnp.float32) * width
    if len(cuts) > 0:
        drawn = block_levels(stream_key, shape, cuts, -0.22, 0.18) * drawn
    return jnp.clip(drawn, min=-reach, max=reach).astype(held_as)


def setup_inputs(seed: int = 0, part: int = 0) -> dict:
    splits = jax.random.split(jax.random.key(seed), 15)
    part_keys = jax.random.split(jax.random.fold_in(splits[14], part), 15)
    queries = draw_queries(jax.random.fold_in(jax.random.fold_in(splits[14], part), 71), part)
    residual = normal_values(part_keys[1], (ROWS, D), 1.0, 6.0, ((0, 16),))
    new_keys = normal_values(part_keys[2], (ROWS, KVD), 1.0, 6.0, ((0, 16),))
    new_values = normal_values(part_keys[3], (ROWS, KVD), 1.0, 6.0, ((0, 16),))
    key_pool = draw_key_pool(jax.random.fold_in(jax.random.fold_in(splits[14], part), 71), part)
    value_pool = normal_values(part_keys[5], (N_ATTN * PAGES_DEV, PAGE, KVD), 1.0, 6.0, ((0, 16),))
    page_table = draw_page_table(jax.random.fold_in(jax.random.fold_in(splits[14], part), 71), part)
    lengths = with_ends(jax.random.randint(part_keys[7], (ROWS,), 2, S), jax.random.fold_in(part_keys[7], 1), 2, S - 1).astype(jnp.int32)
    migrate = draw_migrate(jax.random.fold_in(jax.random.fold_in(splits[14], part), 71), part)
    chosen = draw_chosen(jax.random.fold_in(jax.random.fold_in(splits[14], part), 71), part)
    router_weight = normal_values(splits[10], (D, EXPERTS), D ** -0.5, 0.078125)
    w_gate = normal_values(splits[11], (D, EXP_ON * FFW), D ** -0.5, 0.078125, ((1, 16),))
    w_up = normal_values(splits[12], (D, EXP_ON * FFW), D ** -0.5, 0.078125, ((1, 16),))
    w_down = normal_values(splits[13], (EXP_ON * FFW, D), FFW ** -0.5, 0.1875, ((0, 16),))
    return dict(queries=queries, residual=residual, new_keys=new_keys, new_values=new_values, key_pool=key_pool, value_pool=value_pool, page_table=page_table, lengths=lengths, migrate=migrate, chosen=chosen, router_weight=router_weight, w_gate=w_gate, w_up=w_up, w_down=w_down)


def build_sequence(pool_pages, table_rows, lengths_here, fresh_rows):
    gathered = jnp.take(pool_pages, table_rows, axis=0)
    sequence = gathered.reshape(table_rows.shape[0], -1, pool_pages.shape[-1])
    positions = jnp.arange(sequence.shape[1], dtype=jnp.int32)[None, :, None]
    boundary = lengths_here[:, None, None]
    sequence = jnp.where(positions < boundary, sequence, jnp.zeros_like(sequence))
    return jnp.where(positions == boundary, fresh_rows[:, None, :], sequence)

def attend(query_rows, key_rows, value_rows, lengths_here):
    row_count = query_rows.shape[0]
    kv_count = key_rows.shape[-1] // HEAD_DIM
    group_size = query_rows.shape[-1] // key_rows.shape[-1]
    position_count = key_rows.shape[1]
    query_split = query_rows.reshape(row_count, kv_count, group_size, HEAD_DIM).astype(jnp.float32)
    key_split = key_rows.reshape(row_count, position_count, kv_count, HEAD_DIM).astype(jnp.float32)
    value_split = value_rows.reshape(row_count, position_count, kv_count, HEAD_DIM).astype(jnp.float32)
    scores = jnp.einsum('rkgd,rskd->rkgs', query_split, key_split) / math.sqrt(HEAD_DIM)
    positions = jnp.arange(position_count, dtype=jnp.int32)
    visible = positions[None, None, None, :] <= lengths_here[:, None, None, None]
    scores = jnp.where(visible, scores, -jnp.inf)
    highest = lax.optimization_barrier(jnp.max(scores, axis=-1, keepdims=True))
    exponent = jnp.where(visible, jnp.exp(scores - highest), 0.0)
    probs = (exponent / lax.optimization_barrier(jnp.sum(exponent, axis=-1, keepdims=True))).astype(jnp.bfloat16)
    attended = jnp.einsum('rkgs,rskd->rkgd', probs.astype(jnp.float32), value_split)
    return attended.reshape(row_count, -1).astype(jnp.bfloat16)

def gate_weights(normed, router_weight, chosen):
    logits = jnp.dot(normed, router_weight, preferred_element_type=jnp.float32)
    first_logit = jnp.take_along_axis(logits, chosen[:, 0:1], axis=1)[:, 0]
    second_logit = jnp.take_along_axis(logits, chosen[:, 1:2], axis=1)[:, 0]
    first_weight = 1.0 / (1.0 + jnp.exp(second_logit - first_logit))
    second_weight = 1.0 / (1.0 + jnp.exp(first_logit - second_logit))
    stacked = []
    for expert in range(EXP_ON):
        stacked.append(jnp.where(chosen[:, 0] == expert, first_weight, 0.0) + jnp.where(chosen[:, 1] == expert, second_weight, 0.0))
    return jnp.stack(stacked, axis=0)

def slot_table(chosen, slot_count):
    expert_ids = jnp.arange(EXP_ON, dtype=jnp.int32)[:, None]
    wanted = (chosen[None, :, 0] == expert_ids) | (chosen[None, :, 1] == expert_ids)
    position_of = jnp.cumsum(wanted.astype(jnp.int32), axis=1) - 1
    slot_ids = jnp.arange(slot_count, dtype=jnp.int32)[None, :, None]
    selector = wanted[:, None, :] & (position_of[:, None, :] == slot_ids)
    return (wanted, position_of, selector)

def unpack(expert_sums, wanted, position_of, weights_here):
    accumulated = jnp.zeros((wanted.shape[1], expert_sums.shape[-1]), jnp.float32)
    for expert in range(expert_sums.shape[0]):
        index_rows = jnp.clip(position_of[expert], 0, expert_sums.shape[1] - 1)
        picked = jnp.take(expert_sums[expert], index_rows, axis=0)
        factor = jnp.where(wanted[expert], weights_here[expert], 0.0)
        accumulated = accumulated + factor[:, None] * picked
    return accumulated

def reference(queries, residual, new_keys, new_values, key_pool, value_pool, page_table, lengths, migrate, chosen, router_weight, w_gate, w_up, w_down):
    kv_width = KV_HEADS * HEAD_DIM

    def per_device(inputs):
        query_rows, keys_pool, values_pool, table_rows, lengths_here, fresh_keys, fresh_values, leaving = inputs
        key_seq = build_sequence(keys_pool, table_rows, lengths_here, fresh_keys)
        value_seq = build_sequence(values_pool, table_rows, lengths_here, fresh_values)
        attended = attend(query_rows, key_seq, value_seq, lengths_here)
        return (attended, jnp.take(key_seq, leaving, axis=0), jnp.take(value_seq, leaving, axis=0))
    inputs = (queries.reshape(N_ATTN, REQ_DEV, D), key_pool.reshape(N_ATTN, PAGES_DEV, PAGE, kv_width), value_pool.reshape(N_ATTN, PAGES_DEV, PAGE, kv_width), page_table.reshape(N_ATTN, REQ_DEV, MAXP), lengths.reshape(N_ATTN, REQ_DEV), new_keys.reshape(N_ATTN, REQ_DEV, kv_width), new_values.reshape(N_ATTN, REQ_DEV, kv_width), migrate.reshape(N_ATTN, MIGC))
    attended, leave_keys, leave_values = lax.map(per_device, inputs)
    moved_keys = jnp.roll(leave_keys, 1, axis=0).reshape(MOVED, S, kv_width)
    moved_values = jnp.roll(leave_values, 1, axis=0).reshape(MOVED, S, kv_width)
    state = residual.astype(jnp.float32) + attended.reshape(ROWS, D).astype(jnp.float32)
    normed = (state * lax.rsqrt(lax.optimization_barrier(jnp.mean(state * state, axis=1, keepdims=True)) + 1e-05)).astype(jnp.bfloat16)
    weights_all = gate_weights(normed, router_weight, chosen)
    wanted, position_of, selector = jax.vmap(lambda block_rows: slot_table(block_rows, CAP))(chosen.reshape(N_ATTN, REQ_DEV, 2))
    packed = jnp.einsum('necr,nrd->necd', selector.astype(jnp.float32), normed.reshape(N_ATTN, REQ_DEV, D).astype(jnp.float32)).astype(jnp.bfloat16)
    outputs_list = []
    for expert in range(EXP_ON):
        rows_here = packed[:, expert].reshape(N_ATTN * CAP, D)
        gate_part = jnp.dot(rows_here, w_gate[:, expert * FFW:(expert + 1) * FFW], preferred_element_type=jnp.float32)
        up_part = jnp.dot(rows_here, w_up[:, expert * FFW:(expert + 1) * FFW], preferred_element_type=jnp.float32)
        hidden_units = (jax.nn.silu(gate_part) * up_part).astype(jnp.bfloat16)
        expert_out = jnp.dot(hidden_units, w_down[expert * FFW:(expert + 1) * FFW], preferred_element_type=jnp.float32)
        outputs_list.append(expert_out.reshape(N_ATTN, CAP, D))
    expert_sums = jnp.stack(outputs_list, axis=1)
    device_weights = weights_all.reshape(EXP_ON, N_ATTN, REQ_DEV).transpose(1, 0, 2)
    addition = jax.vmap(unpack)(expert_sums, wanted, position_of, device_weights)
    mixed = (state + addition.reshape(ROWS, D)).astype(jnp.bfloat16)
    return (mixed, moved_keys, moved_values)
```

```python
import math

import jax
import jax.numpy as jnp
from jax import lax
from jax.experimental import pallas as pl
from jax.experimental.pallas import tpu as pltpu
from jax.sharding import PartitionSpec as P

HEAD_DIM = 128
CAP = 5
EXP_ON = 2
F32 = jnp.float32
BF16 = jnp.bfloat16

SMEM = pl.BlockSpec(memory_space=pltpu.SMEM)
VMEM = pl.BlockSpec(memory_space=pltpu.VMEM)
ANY = pl.BlockSpec(memory_space=pl.ANY)


def exchanged(array, mask):
    length = lax.axis_size("attn")
    return lax.ppermute(array, "attn", [(i, i ^ mask) for i in range(length)])


def migrate_kernel(table, lengths, migrate, new_keys, new_values, key_pool, value_pool,
                   out_keys, out_values, fresh, sems):
    moves, positions, _ = out_keys.shape
    page = key_pool.shape[1]
    pages = positions // page
    sides = ((key_pool, out_keys), (value_pool, out_values))
    for m in range(moves):
        request = migrate[m]
        for p in range(pages):
            number = table[request, p]
            for side, (pool, out) in enumerate(sides):
                pltpu.make_async_copy(
                    pool.at[number], out.at[m, pl.ds(p * page, page)], sems.at[side, m]
                ).start()
    fresh[0] = new_keys[...].astype(F32)
    fresh[1] = new_values[...].astype(F32)
    for m in range(moves):
        request = migrate[m]
        length = lengths[request]
        for side, (pool, out) in enumerate(sides):
            pltpu.make_async_copy(out.at[m], out.at[m], sems.at[side, m]).wait()
            row = fresh[side, pl.ds(request, 1), :]
            for p in range(pages):
                block = out[m, pl.ds(p * page, page), :].astype(F32)
                at = lax.broadcasted_iota(jnp.int32, block.shape, 0) + p * page
                block = jnp.where(at < length, block, jnp.where(at == length, row, 0.0))
                out[m, pl.ds(p * page, page), :] = block.astype(BF16)


def leaving(page_table, lengths, migrate, new_keys, new_values, key_pool, value_pool):
    rows, width = new_keys.shape
    moves = migrate.shape[0]
    positions = page_table.shape[1] * key_pool.shape[1]
    shape = jax.ShapeDtypeStruct((moves, positions, width), BF16)
    return pl.pallas_call(
        migrate_kernel,
        out_shape=(shape, shape),
        in_specs=[SMEM] * 3 + [VMEM] * 2 + [ANY] * 2,
        out_specs=(VMEM, VMEM),
        scratch_shapes=[pltpu.VMEM((2, rows, width), F32), pltpu.SemaphoreType.DMA((2, moves))],
        compiler_params=pltpu.CompilerParams(vmem_limit_bytes=8 << 20),
        cost_estimate=pl.CostEstimate(flops=0, bytes_accessed=4 << 20, transcendentals=0),
    )(page_table, lengths, migrate, new_keys, new_values, key_pool, value_pool)


def attend_kernel(table, lengths, chosen, mine, queries, residual, new_keys, new_values,
                  key_pool, value_pool, state_out, normed_out, own_out, away_out,
                  keys, values, heads_q, heads_r, fresh, sems):
    rows, width = queries.shape
    page = key_pool.shape[1]
    positions = keys.shape[1]
    pages = positions // page
    kv_width = keys.shape[2]
    kv_heads = kv_width // HEAD_DIM
    heads = width // HEAD_DIM
    group = heads // kv_heads
    for r in range(rows):
        for p in range(pages):
            number = table[r, p]
            at = pl.ds(p * page, page)
            pltpu.make_async_copy(key_pool.at[number], keys.at[r, at], sems.at[0, r]).start()
            pltpu.make_async_copy(value_pool.at[number], values.at[r, at], sems.at[1, r]).start()
    fresh[0] = new_keys[...].astype(F32)
    fresh[1] = new_values[...].astype(F32)
    for h in range(heads):
        cols = slice(h * HEAD_DIM, (h + 1) * HEAD_DIM)
        heads_q[pl.ds(h, rows, stride=heads), :] = queries[:, cols].astype(F32)
        heads_r[pl.ds(h, rows, stride=heads), :] = residual[:, cols].astype(F32)
    own_out[...] = jnp.zeros_like(own_out)
    away_out[...] = jnp.zeros_like(away_out)
    head_of = lax.broadcasted_iota(jnp.int32, (heads, HEAD_DIM), 0)
    at_of = lax.broadcasted_iota(jnp.int32, (heads, positions), 1)
    in_group = [(head_of >= g * group) & (head_of < (g + 1) * group) for g in range(kv_heads)]
    expert = mine[0]
    taken = [jnp.int32(0), jnp.int32(0)]
    for r in range(rows):
        length = lengths[r]
        first = pl.multiple_of(length // page * page, page)
        tail = pl.ds(first, page)
        here = lax.broadcasted_iota(jnp.int32, (page, kv_width), 0) == length - first
        for side, buffer in enumerate((keys, values)):
            pltpu.make_async_copy(buffer.at[r], buffer.at[r], sems.at[side, r]).wait()
            block = buffer[r, tail, :].astype(F32)
            block = jnp.where(here, fresh[side, r:r + 1, :], block)
            buffer[r, tail, :] = block.astype(BF16)
        query = heads_q[r * heads:(r + 1) * heads, :]
        spread = jnp.concatenate(
            [jnp.where(inside, query, 0.0).astype(BF16) for inside in in_group], axis=1
        )
        scores = lax.dot_general(
            spread, keys[r], (((1,), (1,)), ((), ())), preferred_element_type=F32
        ) * (1.0 / math.sqrt(HEAD_DIM))
        visible = at_of <= length
        scores = jnp.where(visible, scores, -jnp.inf)
        highest = jnp.max(scores, axis=1, keepdims=True)
        exponent = jnp.where(visible, jnp.exp(scores - highest), 0.0)
        probs = (exponent / jnp.sum(exponent, axis=1, keepdims=True)).astype(BF16)
        mixed = jnp.dot(probs, values[r], preferred_element_type=F32)
        attended = mixed[:, :HEAD_DIM]
        for g in range(1, kv_heads):
            attended = jnp.where(
                in_group[g], mixed[:, g * HEAD_DIM:(g + 1) * HEAD_DIM], attended
            )
        state = heads_r[r * heads:(r + 1) * heads, :] + attended.astype(BF16).astype(F32)
        state_out[r] = state
        square = jnp.sum(jnp.sum(state * state, axis=1, keepdims=True), axis=0, keepdims=True)
        normed = (state * lax.rsqrt(square / width + 1e-05)).astype(BF16)
        normed_out[r] = normed
        for side, (out, number) in enumerate(((own_out, expert), (away_out, 1 - expert))):
            wanted = (chosen[r, 0] == number) | (chosen[r, 1] == number)
            slot = jnp.minimum(taken[side], CAP - 1)

            @pl.when(wanted)
            def _():
                out[slot] = normed

            taken[side] = taken[side] + wanted.astype(jnp.int32)


def attended(page_table, lengths, chosen, mine, queries, residual, new_keys, new_values,
             key_pool, value_pool):
    rows, width = queries.shape
    heads = width // HEAD_DIM
    kv_width = new_keys.shape[1]
    positions = page_table.shape[1] * key_pool.shape[1]
    packed = jax.ShapeDtypeStruct((CAP, heads, HEAD_DIM), BF16)
    return pl.pallas_call(
        attend_kernel,
        out_shape=(
            jax.ShapeDtypeStruct((rows, heads, HEAD_DIM), F32),
            jax.ShapeDtypeStruct((rows, heads, HEAD_DIM), BF16),
            packed,
            packed,
        ),
        in_specs=[SMEM] * 4 + [VMEM] * 4 + [ANY] * 2,
        out_specs=(VMEM,) * 4,
        scratch_shapes=[
            pltpu.VMEM((rows, positions, kv_width), BF16),
            pltpu.VMEM((rows, positions, kv_width), BF16),
            pltpu.VMEM((rows * heads, HEAD_DIM), F32),
            pltpu.VMEM((rows * heads, HEAD_DIM), F32),
            pltpu.VMEM((2, rows, kv_width), F32),
            pltpu.SemaphoreType.DMA((2, rows)),
        ],
        compiler_params=pltpu.CompilerParams(vmem_limit_bytes=16 << 20),
        cost_estimate=pl.CostEstimate(
            flops=400_000_000, bytes_accessed=36 << 20, transcendentals=1 << 17
        ),
    )(page_table, lengths, chosen, mine, queries, residual, new_keys, new_values,
      key_pool, value_pool)


def expert_kernel(kept_rows, given_rows, w_gate, w_up, w_down, kept, given, split, flat, back):
    block, heads, _ = kept_rows.shape
    half = block * heads
    split[:half] = kept_rows[...].astype(F32).reshape(half, HEAD_DIM)
    split[half:] = given_rows[...].astype(F32).reshape(half, HEAD_DIM)
    for h in range(heads):
        cols = slice(h * HEAD_DIM, (h + 1) * HEAD_DIM)
        flat[:, cols] = split[pl.ds(h, 2 * block, stride=heads), :].astype(BF16)
    gate = jnp.dot(flat[...], w_gate[...], preferred_element_type=F32)
    up = jnp.dot(flat[...], w_up[...], preferred_element_type=F32)
    hidden = (gate / (1.0 + jnp.exp(-gate)) * up).astype(BF16)
    wide = 4
    for first in range(0, heads, wide):
        cols = slice(first * HEAD_DIM, (first + wide) * HEAD_DIM)
        part = jnp.dot(hidden, w_down[:, cols], preferred_element_type=F32)
        for h in range(wide):
            back[pl.ds(first + h, 2 * block, stride=heads), :] = part[
                :, h * HEAD_DIM:(h + 1) * HEAD_DIM
            ]
    kept[...] = back[:half].reshape(block, heads, HEAD_DIM)
    given[...] = back[half:].reshape(block, heads, HEAD_DIM).astype(BF16)


def expert_parts(kept_rows, given_rows, w_gate, w_up, w_down):
    total, heads, _ = kept_rows.shape
    block = 8 * CAP
    if total % block:
        block = CAP
    rows = pl.BlockSpec((block, heads, HEAD_DIM), lambda i: (i, 0, 0))

    def fixed(array):
        return pl.BlockSpec(array.shape, lambda i: (0, 0))

    return pl.pallas_call(
        expert_kernel,
        grid=(total // block,),
        out_shape=(
            jax.ShapeDtypeStruct(kept_rows.shape, F32),
            jax.ShapeDtypeStruct(kept_rows.shape, BF16),
        ),
        in_specs=[rows, rows, fixed(w_gate), fixed(w_up), fixed(w_down)],
        out_specs=(rows, rows),
        scratch_shapes=[
            pltpu.VMEM((2 * block * heads, HEAD_DIM), F32),
            pltpu.VMEM((2 * block, heads * HEAD_DIM), BF16),
            pltpu.VMEM((2 * block * heads, HEAD_DIM), F32),
        ],
        compiler_params=pltpu.CompilerParams(vmem_limit_bytes=32 << 20),
        cost_estimate=pl.CostEstimate(
            flops=400_000_000, bytes_accessed=8 << 20, transcendentals=10240
        ),
    )(kept_rows, given_rows, w_gate, w_up, w_down)


def finish_kernel(chosen, mine, weights, state, own, away, mixed, rows_split):
    rows, heads, _ = state.shape
    expert = mine[0]
    taken = [jnp.int32(0), jnp.int32(0)]
    for r in range(rows):
        total = state[r]
        for side, (sums, number) in enumerate(((own, expert), (away, 1 - expert))):
            wanted = (chosen[r, 0] == number) | (chosen[r, 1] == number)
            slot = jnp.minimum(taken[side], CAP - 1)
            factor = jnp.where(wanted, weights[number, r], 0.0)
            total = total + factor * sums[slot].astype(F32)
            taken[side] = taken[side] + wanted.astype(jnp.int32)
        rows_split[r * heads:(r + 1) * heads, :] = total
    for h in range(heads):
        mixed[:, h * HEAD_DIM:(h + 1) * HEAD_DIM] = rows_split[
            pl.ds(h, rows, stride=heads), :
        ].astype(BF16)


def finished(chosen, mine, weights, state, own, away):
    rows, heads, _ = state.shape
    return pl.pallas_call(
        finish_kernel,
        out_shape=jax.ShapeDtypeStruct((rows, heads * HEAD_DIM), BF16),
        in_specs=[SMEM] * 3 + [VMEM] * 3,
        out_specs=VMEM,
        scratch_shapes=[pltpu.VMEM((rows * heads, HEAD_DIM), F32)],
        compiler_params=pltpu.CompilerParams(vmem_limit_bytes=8 << 20),
    )(chosen, mine, weights, state, own, away)


def gate_weights(normed, router_weight, chosen):
    rows, heads, _ = normed.shape
    router = router_weight.reshape(heads, HEAD_DIM, -1)
    logits = jnp.einsum("rhd,hde->re", normed, router, preferred_element_type=F32)
    numbers = jnp.arange(logits.shape[1], dtype=jnp.int32)[None, :]
    first = chosen[:, 0:1]
    second = chosen[:, 1:2]
    first_logit = jnp.sum(jnp.where(numbers == first, logits, 0.0), axis=1, keepdims=True)
    second_logit = jnp.sum(jnp.where(numbers == second, logits, 0.0), axis=1, keepdims=True)
    first_weight = 1.0 / (1.0 + jnp.exp(second_logit - first_logit))
    second_weight = 1.0 / (1.0 + jnp.exp(first_logit - second_logit))
    experts = jnp.arange(EXP_ON, dtype=jnp.int32)[None, :]
    weights = jnp.where(first == experts, first_weight, 0.0) + jnp.where(
        second == experts, second_weight, 0.0
    )
    return weights.T


def body(
    queries,
    residual,
    new_keys,
    new_values,
    key_pool,
    value_pool,
    page_table,
    lengths,
    migrate,
    chosen,
    router_weight,
    w_gate,
    w_up,
    w_down,
):
    length = lax.axis_size("attn")
    swap = length // 2
    masks = list(range(2, swap, 2))
    mine = (lax.axis_index("attn") // (length // EXP_ON)).astype(jnp.int32).reshape(1)
    along = [(i, (i + 1) % length) for i in range(length)]
    leave_keys, leave_values = leaving(
        page_table, lengths, migrate, new_keys, new_values, key_pool, value_pool
    )
    arrived_keys = lax.ppermute(leave_keys, "attn", along)
    arrived_values = lax.ppermute(leave_values, "attn", along)
    state, normed, own, away = attended(
        page_table, lengths, chosen, mine, queries, residual, new_keys, new_values,
        key_pool, value_pool,
    )
    weights = gate_weights(normed, router_weight, chosen)
    swapped = exchanged(away, swap)
    blocks = [own] + [exchanged(own, mask) for mask in masks]
    blocks += [swapped] + [exchanged(swapped, mask) for mask in masks]
    mine_rows = jnp.concatenate(blocks)
    other_rows = exchanged(mine_rows, 1)
    kept, given = expert_parts(mine_rows, other_rows, w_gate, w_up, w_down)
    summed = (kept + exchanged(given, 1).astype(F32)).astype(BF16)
    count = len(masks) + 1
    parts = [summed[i * CAP:(i + 1) * CAP] for i in range(2 * count)]
    back = parts[count].astype(F32)
    for i, mask in enumerate(masks):
        back = back + exchanged(parts[count + 1 + i], mask).astype(F32)
    away_sums = exchanged(back.astype(BF16), swap)
    own_sums = parts[0].astype(F32)
    for i, mask in enumerate(masks):
        own_sums = own_sums + exchanged(parts[1 + i], mask).astype(F32)
    mixed = finished(chosen, mine, weights, state, own_sums, away_sums)
    return (mixed, arrived_keys, arrived_values)


def solution(mesh):
    placed = (
        P(("groups", "attn"), None),
        P(("groups", "attn"), None),
        P(("groups", "attn"), None),
        P(("groups", "attn"), None),
        P(("groups", "attn"), None, None),
        P(("groups", "attn"), None, None),
        P(("groups", "attn"), None),
        P(("groups", "attn")),
        P(("groups", "attn")),
        P(("groups", "attn"), None),
        P(),
        P(None, "attn"),
        P(None, "attn"),
        P("attn", None),
    )
    return jax.shard_map(
        body,
        mesh=mesh,
        in_specs=placed,
        out_specs=(
            P(("groups", "attn"), None),
            P(("groups", "attn"), None, None),
            P(("groups", "attn"), None, None),
        ),
        check_vma=False,
    )
```

```python
import math

import jax
import jax.numpy as jnp
from jax import lax
from jax.experimental import pallas as pl
from jax.experimental.pallas import tpu as pltpu
from jax.sharding import PartitionSpec as P

HEAD_DIM = 128
CAP = 5
EXP_ON = 2
F32 = jnp.float32
BF16 = jnp.bfloat16

SMEM = pl.BlockSpec(memory_space=pltpu.SMEM)
VMEM = pl.BlockSpec(memory_space=pltpu.VMEM)
ANY = pl.BlockSpec(memory_space=pl.ANY)
HBM = pl.BlockSpec(memory_space=pltpu.HBM)


def in_hbm(array):
    return pltpu.with_memory_space_constraint(array, pltpu.HBM)


def exchanged(array, mask):
    length = lax.axis_size("attn")
    return lax.ppermute(array, "attn", [(i, i ^ mask) for i in range(length)])


def stage_kernel(table_at, lengths_at, migrate_at, chosen_at, mine, queries_at, residual_at,
                 new_keys_at, new_values_at, key_pool_at, value_pool_at,
                 plan, key_pool, value_pool, heads_q, heads_r, moved_keys, moved_values,
                 table, lengths, migrate, chosen, queries, residual, new_keys, new_values,
                 fresh, small_sems, row_sems, pool_sems):
    pages, rows = table.shape
    page = key_pool.shape[1]
    moves = moved_keys.shape[0]
    heads = heads_q.shape[0] // rows
    small = [
        pltpu.make_async_copy(source, target, small_sems.at[i])
        for i, (source, target) in enumerate(
            ((table_at, table), (lengths_at, lengths), (migrate_at, migrate), (chosen_at, chosen))
        )
    ]
    wide = [
        pltpu.make_async_copy(source, target, row_sems.at[i])
        for i, (source, target) in enumerate(
            ((queries_at, queries), (residual_at, residual),
             (new_keys_at, new_keys), (new_values_at, new_values))
        )
    ]
    pool = []
    cut = key_pool.shape[0] // POOL_CUTS
    for c in range(POOL_CUTS):
        part = pl.ds(c * cut, cut)
        for side, (source, target) in enumerate(
            ((key_pool_at, key_pool), (value_pool_at, value_pool))
        ):
            pool.append(
                pltpu.make_async_copy(source.at[part], target.at[part], pool_sems.at[side, c])
            )
    for copy in wide[:2] + small + wide[2:] + pool:
        copy.start()
    for copy, target, source in zip(wide[:2], (heads_q, heads_r), (queries, residual)):
        copy.wait()
        for h in range(heads):
            target[pl.ds(h, rows, stride=heads), :] = source[
                :, h * HEAD_DIM:(h + 1) * HEAD_DIM
            ].astype(F32)
    for copy in small:
        copy.wait()
    expert = mine[0]
    other = 1 - expert
    taken_own, taken_away = jnp.int32(0), jnp.int32(0)
    own_slots, away_slots = [], []
    for r in range(rows):
        for p in range(pages):
            plan[p, r] = table[p, r]
        plan[pages, r] = lengths[r]
        first, second = chosen[0, r], chosen[1, r]
        own = ((first == expert) | (second == expert)).astype(jnp.int32)
        away = ((first == other) | (second == other)).astype(jnp.int32)
        own_slots.append(jnp.where(own == 1, taken_own, -1))
        away_slots.append(jnp.where(away == 1, taken_away, -1))
        plan[pages + 1, r] = own_slots[r]
        plan[pages + 2, r] = away_slots[r]
        taken_own = taken_own + own
        taken_away = taken_away + away
    behind = taken_away
    for r in range(rows):
        is_away = away_slots[r] >= 0
        plan[pages + 3, jnp.where(is_away, away_slots[r], behind)] = jnp.int32(r)
        behind = behind + jnp.where(is_away, 0, 1)
    plan[pages + 4, 0] = taken_away
    for copy, side in zip(wide[2:], (0, 1)):
        copy.wait()
        fresh[side] = (new_keys, new_values)[side][...].astype(F32)
    for copy in pool:
        copy.wait()
    inside = lax.broadcasted_iota(jnp.int32, (page, key_pool.shape[2]), 0)
    for r in range(rows):
        length = lengths[r]
        last = length // page
        number = table[last, r]
        here = inside == length - last * page
        for side, buffer in enumerate((key_pool, value_pool)):
            block = buffer[number].astype(F32)
            buffer[number] = jnp.where(here, fresh[side, r:r + 1, :], block).astype(BF16)
    for m in range(moves):
        request = migrate[m]
        length = lengths[request]
        for p in range(pages):
            number = table[p, request]
            kept = inside + p * page <= length
            for buffer, out in ((key_pool, moved_keys), (value_pool, moved_values)):
                block = jnp.where(kept, buffer[number].astype(F32), 0.0)
                out[m, p * page:(p + 1) * page, :] = block.astype(BF16)


POOL_CUTS = 3


def staged(page_table, lengths, migrate, chosen, mine, queries, residual, new_keys, new_values,
           key_pool, value_pool):
    rows, width = queries.shape
    heads = width // HEAD_DIM
    kv_width = new_keys.shape[1]
    moves = migrate.shape[0]
    pages = page_table.shape[1]
    moved = jax.ShapeDtypeStruct((moves, pages * key_pool.shape[1], kv_width), BF16)
    split = jax.ShapeDtypeStruct((rows * heads, HEAD_DIM), F32)
    return pl.pallas_call(
        stage_kernel,
        out_shape=(
            jax.ShapeDtypeStruct((pages + 5, rows), jnp.int32),
            jax.ShapeDtypeStruct(key_pool.shape, BF16),
            jax.ShapeDtypeStruct(value_pool.shape, BF16),
            split, split, moved, moved,
        ),
        in_specs=[HBM] * 4 + [SMEM] + [HBM] * 6,
        out_specs=(SMEM,) + (VMEM,) * 6,
        scratch_shapes=[
            pltpu.SMEM((pages, rows), jnp.int32),
            pltpu.SMEM(lengths.shape, jnp.int32),
            pltpu.SMEM(migrate.shape, jnp.int32),
            pltpu.SMEM((2, rows), jnp.int32),
            pltpu.VMEM(queries.shape, BF16),
            pltpu.VMEM(queries.shape, BF16),
            pltpu.VMEM(new_keys.shape, BF16),
            pltpu.VMEM(new_keys.shape, BF16),
            pltpu.VMEM((2, rows, kv_width), F32),
            pltpu.SemaphoreType.DMA((4,)),
            pltpu.SemaphoreType.DMA((4,)),
            pltpu.SemaphoreType.DMA((2, POOL_CUTS)),
        ],
        compiler_params=pltpu.CompilerParams(vmem_limit_bytes=16 << 20),
        cost_estimate=pl.CostEstimate(flops=0, bytes_accessed=8 << 20, transcendentals=0),
    )(*[in_hbm(a) for a in (page_table.T, lengths, migrate, chosen.T)], mine,
      *[in_hbm(a) for a in (queries, residual, new_keys, new_values, key_pool, value_pool)])


def attend_pair(plan, pair, key_pool, value_pool, heads_q, heads_r, state_out, normed_out):
    page = key_pool.shape[1]
    kv_heads = key_pool.shape[2] // HEAD_DIM
    rows, heads, _ = state_out.shape
    group = heads // kv_heads
    pages = plan.shape[0] - 5
    positions = pages * page
    head_of = lax.broadcasted_iota(jnp.int32, (heads, HEAD_DIM), 0)
    at_of = lax.broadcasted_iota(jnp.int32, (heads, positions), 1)
    in_group = [(head_of >= g * group) & (head_of < (g + 1) * group) for g in range(kv_heads)]
    both = [plan[pages + 3, 2 * pair + i] for i in range(2)]
    starts = [pl.multiple_of(r * heads, 8) for r in both]
    numbers = [[plan[p, r] for p in range(pages)] for r in both]
    queries = [heads_q[pl.ds(start, heads), :] for start in starts]
    spread = [
        jnp.concatenate(
            [jnp.where(inside, query, 0.0).astype(BF16) for inside in in_group], axis=1
        )
        for query in queries
    ]
    scores = [
        lax.dot_general(
            rows_q, jnp.concatenate([key_pool[n] for n in number], axis=0),
            (((1,), (1,)), ((), ())), preferred_element_type=F32,
        ) * (1.0 / math.sqrt(HEAD_DIM))
        for rows_q, number in zip(spread, numbers)
    ]
    visible = [at_of <= plan[pages, r] for r in both]
    scores = [jnp.where(seen, score, -jnp.inf) for seen, score in zip(visible, scores)]
    highest = [jnp.max(score, axis=1, keepdims=True) for score in scores]
    exponent = [
        jnp.where(seen, jnp.exp(score - high), 0.0)
        for seen, score, high in zip(visible, scores, highest)
    ]
    sums = [jnp.sum(e, axis=1, keepdims=True) for e in exponent]
    probs = [(e / s).astype(BF16) for e, s in zip(exponent, sums)]
    mixed = [
        jnp.dot(
            prob, jnp.concatenate([value_pool[n] for n in number], axis=0),
            preferred_element_type=F32,
        )
        for prob, number in zip(probs, numbers)
    ]
    states = []
    for start, mix in zip(starts, mixed):
        attended = mix[:, :HEAD_DIM]
        for g in range(1, kv_heads):
            attended = jnp.where(in_group[g], mix[:, g * HEAD_DIM:(g + 1) * HEAD_DIM], attended)
        states.append(heads_r[pl.ds(start, heads), :] + attended.astype(BF16).astype(F32))
    squares = [
        jnp.sum(jnp.sum(state * state, axis=1, keepdims=True), axis=0, keepdims=True)
        for state in states
    ]
    normed = [
        (state * lax.rsqrt(square / (heads * HEAD_DIM) + 1e-05)).astype(BF16)
        for state, square in zip(states, squares)
    ]
    for r, state, rows_n in zip(both, states, normed):
        state_out[r] = state
        normed_out[r] = rows_n
    return both, normed


def away_kernel(plan, key_pool, value_pool, heads_q, heads_r,
                state_out, normed_out, own_out, away_out):
    pages = plan.shape[0] - 5
    own_out[...] = jnp.zeros_like(own_out)
    away_out[...] = jnp.zeros_like(away_out)

    def step(pair, carry):
        both, normed = attend_pair(
            plan, pair, key_pool, value_pool, heads_q, heads_r, state_out, normed_out
        )
        for r, rows_n in zip(both, normed):
            for row, out in ((pages + 1, own_out), (pages + 2, away_out)):
                slot = plan[row, r]

                @pl.when(slot >= 0)
                def _():
                    out[jnp.clip(slot, 0, CAP - 1)] = rows_n

        return carry

    lax.fori_loop(0, (plan[pages + 4, 0] + 1) // 2, step, 0)


def rest_kernel(plan, key_pool, value_pool, heads_q, heads_r, state_in, normed_in, own_in,
                state_out, normed_out, own_out):
    pages = plan.shape[0] - 5
    rows = state_out.shape[0]
    state_out[...] = state_in[...]
    normed_out[...] = normed_in[...]
    own_out[...] = own_in[...]

    def step(pair, carry):
        both, normed = attend_pair(
            plan, pair, key_pool, value_pool, heads_q, heads_r, state_out, normed_out
        )
        for r, rows_n in zip(both, normed):
            slot = plan[pages + 1, r]

            @pl.when(slot >= 0)
            def _():
                own_out[jnp.clip(slot, 0, CAP - 1)] = rows_n

        return carry

    lax.fori_loop((plan[pages + 4, 0] + 1) // 2, rows // 2, step, 0)


def attend_shapes(rows, heads):
    packed = jax.ShapeDtypeStruct((CAP, heads, HEAD_DIM), BF16)
    return (
        jax.ShapeDtypeStruct((rows, heads, HEAD_DIM), F32),
        jax.ShapeDtypeStruct((rows, heads, HEAD_DIM), BF16),
        packed,
        packed,
    )


def attended_away(plan, key_pool, value_pool, heads_q, heads_r):
    rows = plan.shape[1]
    heads = heads_q.shape[0] // rows
    return pl.pallas_call(
        away_kernel,
        out_shape=attend_shapes(rows, heads),
        in_specs=[SMEM] + [VMEM] * 4,
        out_specs=(VMEM,) * 4,
        compiler_params=pltpu.CompilerParams(vmem_limit_bytes=8 << 20),
        cost_estimate=pl.CostEstimate(
            flops=1 << 27, bytes_accessed=8 << 20, transcendentals=1 << 15
        ),
    )(plan, key_pool, value_pool, heads_q, heads_r)


def attended_rest(plan, key_pool, value_pool, heads_q, heads_r, state, normed, own):
    rows, heads, _ = state.shape
    return pl.pallas_call(
        rest_kernel,
        out_shape=attend_shapes(rows, heads)[:3],
        in_specs=[SMEM] + [VMEM] * 7,
        out_specs=(VMEM,) * 3,
        compiler_params=pltpu.CompilerParams(vmem_limit_bytes=8 << 20),
        cost_estimate=pl.CostEstimate(
            flops=1 << 28, bytes_accessed=24 << 20, transcendentals=1 << 16
        ),
    )(plan, key_pool, value_pool, heads_q, heads_r, state, normed, own)


def expert_kernel(kept_rows, given_rows, w_gate, w_up, w_down, arrived_keys, arrived_values,
                  kept, given, moved_keys, moved_values, split, flat, back, sems):
    copies = [
        pltpu.make_async_copy(arrived_keys, moved_keys, sems.at[0]),
        pltpu.make_async_copy(arrived_values, moved_values, sems.at[1]),
    ]

    @pl.when(pl.program_id(0) == 0)
    def _():
        for copy in copies:
            copy.start()

    block, heads, _ = kept_rows.shape
    half = block * heads
    split[:half] = kept_rows[...].astype(F32).reshape(half, HEAD_DIM)
    split[half:] = given_rows[...].astype(F32).reshape(half, HEAD_DIM)
    for h in range(heads):
        cols = slice(h * HEAD_DIM, (h + 1) * HEAD_DIM)
        flat[:, cols] = split[pl.ds(h, 2 * block, stride=heads), :].astype(BF16)
    gate = jnp.dot(flat[...], w_gate[...], preferred_element_type=F32)
    up = jnp.dot(flat[...], w_up[...], preferred_element_type=F32)
    hidden = (gate / (1.0 + jnp.exp(-gate)) * up).astype(BF16)
    wide = 4
    for first in range(0, heads, wide):
        cols = slice(first * HEAD_DIM, (first + wide) * HEAD_DIM)
        part = jnp.dot(hidden, w_down[:, cols], preferred_element_type=F32)
        for h in range(wide):
            back[pl.ds(first + h, 2 * block, stride=heads), :] = part[
                :, h * HEAD_DIM:(h + 1) * HEAD_DIM
            ]
    kept[...] = back[:half].reshape(block, heads, HEAD_DIM)
    given[...] = back[half:].reshape(block, heads, HEAD_DIM).astype(BF16)

    @pl.when(pl.program_id(0) == pl.num_programs(0) - 1)
    def _():
        for copy in copies:
            copy.wait()


def expert_parts(kept_rows, given_rows, w_gate, w_up, w_down, arrived_keys, arrived_values):
    total, heads, _ = kept_rows.shape
    block = 8 * CAP
    if total % block:
        block = CAP
    rows = pl.BlockSpec((block, heads, HEAD_DIM), lambda i: (i, 0, 0))

    def fixed(array):
        return pl.BlockSpec(array.shape, lambda i: (0, 0))

    return pl.pallas_call(
        expert_kernel,
        grid=(total // block,),
        out_shape=(
            jax.ShapeDtypeStruct(kept_rows.shape, F32),
            jax.ShapeDtypeStruct(kept_rows.shape, BF16),
            jax.ShapeDtypeStruct(arrived_keys.shape, BF16),
            jax.ShapeDtypeStruct(arrived_values.shape, BF16),
        ),
        in_specs=[rows, rows, fixed(w_gate), fixed(w_up), fixed(w_down), ANY, ANY],
        out_specs=(rows, rows, HBM, HBM),
        scratch_shapes=[
            pltpu.VMEM((2 * block * heads, HEAD_DIM), F32),
            pltpu.VMEM((2 * block, heads * HEAD_DIM), BF16),
            pltpu.VMEM((2 * block * heads, HEAD_DIM), F32),
            pltpu.SemaphoreType.DMA((2,)),
        ],
        compiler_params=pltpu.CompilerParams(vmem_limit_bytes=32 << 20),
        cost_estimate=pl.CostEstimate(
            flops=400_000_000, bytes_accessed=8 << 20, transcendentals=10240
        ),
    )(kept_rows, given_rows, w_gate, w_up, w_down, arrived_keys, arrived_values)


def finish_kernel(plan, mine, weights, state, own, away, mixed, rows_split):
    rows, heads, _ = state.shape
    pages = plan.shape[0] - 5
    expert = mine[0]
    for r in range(rows):
        total = state[r]
        for row, sums, number in ((pages + 1, own, expert), (pages + 2, away, 1 - expert)):
            slot = plan[row, r]
            factor = jnp.where(slot >= 0, weights[number, r], 0.0)
            total = total + factor * sums[jnp.clip(slot, 0, CAP - 1)].astype(F32)
        rows_split[r * heads:(r + 1) * heads, :] = total
    for h in range(heads):
        mixed[:, h * HEAD_DIM:(h + 1) * HEAD_DIM] = rows_split[
            pl.ds(h, rows, stride=heads), :
        ].astype(BF16)


def finished(plan, mine, weights, state, own, away):
    rows, heads, _ = state.shape
    return pl.pallas_call(
        finish_kernel,
        out_shape=jax.ShapeDtypeStruct((rows, heads * HEAD_DIM), BF16),
        in_specs=[SMEM] * 3 + [VMEM] * 3,
        out_specs=VMEM,
        scratch_shapes=[pltpu.VMEM((rows * heads, HEAD_DIM), F32)],
        compiler_params=pltpu.CompilerParams(vmem_limit_bytes=8 << 20),
    )(plan, mine, weights, state, own, away)


def gate_weights(normed, router_weight, chosen):
    rows, heads, _ = normed.shape
    router = router_weight.reshape(heads, HEAD_DIM, -1)
    logits = jnp.einsum("rhd,hde->re", normed, router, preferred_element_type=F32)
    numbers = jnp.arange(logits.shape[1], dtype=jnp.int32)[None, :]
    first = chosen[:, 0:1]
    second = chosen[:, 1:2]
    first_logit = jnp.sum(jnp.where(numbers == first, logits, 0.0), axis=1, keepdims=True)
    second_logit = jnp.sum(jnp.where(numbers == second, logits, 0.0), axis=1, keepdims=True)
    first_weight = 1.0 / (1.0 + jnp.exp(second_logit - first_logit))
    second_weight = 1.0 / (1.0 + jnp.exp(first_logit - second_logit))
    experts = jnp.arange(EXP_ON, dtype=jnp.int32)[None, :]
    weights = jnp.where(first == experts, first_weight, 0.0) + jnp.where(
        second == experts, second_weight, 0.0
    )
    return weights.T


def body(
    queries,
    residual,
    new_keys,
    new_values,
    key_pool,
    value_pool,
    page_table,
    lengths,
    migrate,
    chosen,
    router_weight,
    w_gate,
    w_up,
    w_down,
):
    length = lax.axis_size("attn")
    swap = length // 2
    masks = list(range(2, swap, 2))
    mine = (lax.axis_index("attn") // (length // EXP_ON)).astype(jnp.int32).reshape(1)
    along = [(i, (i + 1) % length) for i in range(length)]
    plan, keys, values, heads_q, heads_r, leave_keys, leave_values = staged(
        page_table, lengths, migrate, chosen, mine, queries, residual, new_keys, new_values,
        key_pool, value_pool,
    )
    arrived_keys = lax.ppermute(leave_keys, "attn", along)
    arrived_values = lax.ppermute(leave_values, "attn", along)
    state, normed, own, away = attended_away(plan, keys, values, heads_q, heads_r)
    swapped = exchanged(away, swap)
    state, normed, own = attended_rest(
        plan, keys, values, heads_q, heads_r, state, normed, own
    )
    weights = gate_weights(normed, router_weight, chosen)
    rows_here = jnp.concatenate([own, swapped])
    mine_rows = jnp.concatenate([rows_here] + [exchanged(rows_here, mask) for mask in masks])
    other_rows = exchanged(mine_rows, 1)
    kept, given, moved_keys, moved_values = expert_parts(
        mine_rows, other_rows, w_gate, w_up, w_down, arrived_keys, arrived_values
    )
    summed = (kept + exchanged(given, 1).astype(F32)).astype(BF16)
    sent = 2 * CAP
    back = summed[:sent].astype(F32)
    for i, mask in enumerate(masks):
        at = (i + 1) * sent
        back = back + exchanged(summed[at:at + sent], mask).astype(F32)
    own_sums = back[:CAP]
    away_sums = exchanged(back[CAP:].astype(BF16), swap)
    mixed = finished(plan, mine, weights, state, own_sums, away_sums)
    return (mixed, moved_keys, moved_values)


def solution(mesh):
    placed = (
        P(("groups", "attn"), None),
        P(("groups", "attn"), None),
        P(("groups", "attn"), None),
        P(("groups", "attn"), None),
        P(("groups", "attn"), None, None),
        P(("groups", "attn"), None, None),
        P(("groups", "attn"), None),
        P(("groups", "attn")),
        P(("groups", "attn")),
        P(("groups", "attn"), None),
        P(),
        P(None, "attn"),
        P(None, "attn"),
        P("attn", None),
    )
    return jax.shard_map(
        body,
        mesh=mesh,
        in_specs=placed,
        out_specs=(
            P(("groups", "attn"), None),
            P(("groups", "attn"), None, None),
            P(("groups", "attn"), None, None),
        ),
        check_vma=False,
    )
```

```python
import functools
import math

import jax
import jax.numpy as jnp
from jax import lax
from jax.experimental import pallas as pl
from jax.experimental.pallas import tpu as pltpu
from jax.sharding import PartitionSpec as P

HEAD_DIM = 128
CAP = 5
EXP_ON = 2
F32 = jnp.float32
BF16 = jnp.bfloat16

SMEM = pl.BlockSpec(memory_space=pltpu.SMEM)
VMEM = pl.BlockSpec(memory_space=pltpu.VMEM)
ANY = pl.BlockSpec(memory_space=pl.ANY)
HBM = pl.BlockSpec(memory_space=pltpu.HBM)


def in_hbm(array):
    return pltpu.with_memory_space_constraint(array, pltpu.HBM)


def exchanged(array, mask):
    length = lax.axis_size("attn")
    return lax.ppermute(array, "attn", [(i, i ^ mask) for i in range(length)])


def stage_kernel(table_at, lengths_at, migrate_at, chosen_at, mine, queries_at, residual_at,
                 new_keys_at, new_values_at, key_pool_at, value_pool_at,
                 plan, key_pool, value_pool, heads_q, heads_r, *rest):
    moved, scratch = rest[:len(GROUPS)], rest[len(GROUPS):]
    (table, lengths, migrate, chosen, queries, residual, new_keys, new_values,
     fresh, small_sems, row_sems, pool_sems) = scratch
    pages, rows = table.shape
    page = key_pool.shape[1]
    moves = migrate.shape[0]
    heads = heads_q.shape[0] // rows
    small = [
        pltpu.make_async_copy(source, target, small_sems.at[i])
        for i, (source, target) in enumerate(
            ((table_at, table), (lengths_at, lengths), (migrate_at, migrate), (chosen_at, chosen))
        )
    ]
    wide = [
        pltpu.make_async_copy(source, target, row_sems.at[i])
        for i, (source, target) in enumerate(
            ((queries_at, queries), (residual_at, residual),
             (new_keys_at, new_keys), (new_values_at, new_values))
        )
    ]
    pool = []
    cut = key_pool.shape[0] // POOL_CUTS
    for c in range(POOL_CUTS):
        part = pl.ds(c * cut, cut)
        for side, (source, target) in enumerate(
            ((key_pool_at, key_pool), (value_pool_at, value_pool))
        ):
            pool.append(
                pltpu.make_async_copy(source.at[part], target.at[part], pool_sems.at[side, c])
            )
    for copy in wide[:2] + small + wide[2:] + pool:
        copy.start()
    for copy, target, source in zip(wide[:2], (heads_q, heads_r), (queries, residual)):
        copy.wait()
        for h in range(heads):
            target[pl.ds(h, rows, stride=heads), :] = source[
                :, h * HEAD_DIM:(h + 1) * HEAD_DIM
            ].astype(F32)
    for copy in small:
        copy.wait()
    expert = mine[0]
    other = 1 - expert
    taken_own, taken_away = jnp.int32(0), jnp.int32(0)
    own_slots, away_slots = [], []
    for r in range(rows):
        for p in range(pages):
            plan[p, r] = table[p, r]
        plan[pages, r] = lengths[r]
        first, second = chosen[0, r], chosen[1, r]
        own = ((first == expert) | (second == expert)).astype(jnp.int32)
        away = ((first == other) | (second == other)).astype(jnp.int32)
        own_slots.append(jnp.where(own == 1, taken_own, -1))
        away_slots.append(jnp.where(away == 1, taken_away, -1))
        plan[pages + 1, r] = own_slots[r]
        plan[pages + 2, r] = away_slots[r]
        taken_own = taken_own + own
        taken_away = taken_away + away
    only_own = [
        jnp.where(own_slot >= 0, 1, 0) * jnp.where(away_slot >= 0, 0, 1)
        for own_slot, away_slot in zip(own_slots, away_slots)
    ]
    middle = taken_away
    behind = taken_away + sum(only_own)
    for bound, count in enumerate((taken_away, behind)):
        plan[pages + 4, bound] = (count + 1) // 2
    for r in range(rows):
        is_away = away_slots[r] >= 0
        is_own = only_own[r] == 1
        place = jnp.where(is_away, away_slots[r], jnp.where(is_own, middle, behind))
        plan[pages + 3, place] = jnp.int32(r)
        middle = middle + only_own[r]
        behind = behind + jnp.where(is_away | is_own, 0, 1)
    for copy, side in zip(wide[2:], (0, 1)):
        copy.wait()
        fresh[side] = (new_keys, new_values)[side][...].astype(F32)
    for copy in pool:
        copy.wait()
    inside = lax.broadcasted_iota(jnp.int32, (page, key_pool.shape[2]), 0)
    for r in range(rows):
        length = lengths[r]
        last = length // page
        number = table[last, r]
        here = inside == length - last * page
        for side, buffer in enumerate((key_pool, value_pool)):
            block = buffer[number].astype(F32)
            buffer[number] = jnp.where(here, fresh[side, r:r + 1, :], block).astype(BF16)
    for m in range(moves):
        request = migrate[m]
        length = lengths[request]
        for p in range(pages):
            number = table[p, request]
            kept = inside + p * page <= length
            for side, buffer in enumerate((key_pool, value_pool)):
                group, place = PLACES[side * moves + m]
                block = jnp.where(kept, buffer[number].astype(F32), 0.0)
                moved[group][place, p * page:(p + 1) * page, :] = block.astype(BF16)


POOL_CUTS = 3
GROUPS = ((0, 1), (2, 3))
PLACES = [(g, group.index(i)) for i in range(sum(map(len, GROUPS)))
          for g, group in enumerate(GROUPS) if i in group]
COST = 1 << 20


def staged(page_table, lengths, migrate, chosen, mine, queries, residual, new_keys, new_values,
           key_pool, value_pool):
    rows, width = queries.shape
    heads = width // HEAD_DIM
    kv_width = new_keys.shape[1]
    moves = migrate.shape[0]
    pages = page_table.shape[1]
    moved = tuple(
        jax.ShapeDtypeStruct((len(group), pages * key_pool.shape[1], kv_width), BF16)
        for group in GROUPS
    )
    split = jax.ShapeDtypeStruct((rows * heads, HEAD_DIM), F32)
    return pl.pallas_call(
        stage_kernel,
        out_shape=(
            jax.ShapeDtypeStruct((pages + 5, rows), jnp.int32),
            jax.ShapeDtypeStruct(key_pool.shape, BF16),
            jax.ShapeDtypeStruct(value_pool.shape, BF16),
            split, split,
        ) + moved,
        in_specs=[HBM] * 4 + [SMEM] + [HBM] * 6,
        out_specs=(SMEM,) + (VMEM,) * (4 + len(moved)),
        scratch_shapes=[
            pltpu.SMEM((pages, rows), jnp.int32),
            pltpu.SMEM(lengths.shape, jnp.int32),
            pltpu.SMEM(migrate.shape, jnp.int32),
            pltpu.SMEM((2, rows), jnp.int32),
            pltpu.VMEM(queries.shape, BF16),
            pltpu.VMEM(queries.shape, BF16),
            pltpu.VMEM(new_keys.shape, BF16),
            pltpu.VMEM(new_keys.shape, BF16),
            pltpu.VMEM((2, rows, kv_width), F32),
            pltpu.SemaphoreType.DMA((4,)),
            pltpu.SemaphoreType.DMA((4,)),
            pltpu.SemaphoreType.DMA((2, POOL_CUTS)),
        ],
        compiler_params=pltpu.CompilerParams(vmem_limit_bytes=16 << 20),
        cost_estimate=pl.CostEstimate(flops=0, bytes_accessed=8 << 20, transcendentals=0),
    )(*[in_hbm(a) for a in (page_table.T, lengths, migrate, chosen.T)], mine,
      *[in_hbm(a) for a in (queries, residual, new_keys, new_values, key_pool, value_pool)])


def attend_pair(plan, pair, key_pool, value_pool, heads_q, heads_r, state_out, normed_out):
    page = key_pool.shape[1]
    kv_heads = key_pool.shape[2] // HEAD_DIM
    rows, heads, _ = state_out.shape
    group = heads // kv_heads
    pages = plan.shape[0] - 5
    positions = pages * page
    head_of = lax.broadcasted_iota(jnp.int32, (heads, HEAD_DIM), 0)
    at_of = lax.broadcasted_iota(jnp.int32, (heads, positions), 1)
    in_group = [(head_of >= g * group) & (head_of < (g + 1) * group) for g in range(kv_heads)]
    both = [plan[pages + 3, 2 * pair + i] for i in range(2)]
    starts = [pl.multiple_of(r * heads, 8) for r in both]
    numbers = [[plan[p, r] for p in range(pages)] for r in both]
    queries = [heads_q[pl.ds(start, heads), :] for start in starts]
    spread = [
        jnp.concatenate(
            [jnp.where(inside, query, 0.0).astype(BF16) for inside in in_group], axis=1
        )
        for query in queries
    ]
    scores = [
        lax.dot_general(
            rows_q, jnp.concatenate([key_pool[n] for n in number], axis=0),
            (((1,), (1,)), ((), ())), preferred_element_type=F32,
        ) * (1.0 / math.sqrt(HEAD_DIM))
        for rows_q, number in zip(spread, numbers)
    ]
    visible = [at_of <= plan[pages, r] for r in both]
    scores = [jnp.where(seen, score, -jnp.inf) for seen, score in zip(visible, scores)]
    highest = [jnp.max(score, axis=1, keepdims=True) for score in scores]
    exponent = [
        jnp.where(seen, jnp.exp(score - high), 0.0)
        for seen, score, high in zip(visible, scores, highest)
    ]
    sums = [jnp.sum(e, axis=1, keepdims=True) for e in exponent]
    probs = [(e / s).astype(BF16) for e, s in zip(exponent, sums)]
    mixed = [
        jnp.dot(
            prob, jnp.concatenate([value_pool[n] for n in number], axis=0),
            preferred_element_type=F32,
        )
        for prob, number in zip(probs, numbers)
    ]
    states = []
    for start, mix in zip(starts, mixed):
        attended = mix[:, :HEAD_DIM]
        for g in range(1, kv_heads):
            attended = jnp.where(in_group[g], mix[:, g * HEAD_DIM:(g + 1) * HEAD_DIM], attended)
        states.append(heads_r[pl.ds(start, heads), :] + attended.astype(BF16).astype(F32))
    squares = [
        jnp.sum(jnp.sum(state * state, axis=1, keepdims=True), axis=0, keepdims=True)
        for state in states
    ]
    normed = [
        (state * lax.rsqrt(square / (heads * HEAD_DIM) + 1e-05)).astype(BF16)
        for state, square in zip(states, squares)
    ]
    for r, state, rows_n in zip(both, states, normed):
        state_out[r] = state
        normed_out[r] = rows_n
    return both, normed


def away_kernel(plan, key_pool, value_pool, heads_q, heads_r,
                state_out, normed_out, own_out, away_out):
    pages = plan.shape[0] - 5
    own_out[...] = jnp.zeros_like(own_out)
    away_out[...] = jnp.zeros_like(away_out)

    def step(pair, carry):
        both, normed = attend_pair(
            plan, pair, key_pool, value_pool, heads_q, heads_r, state_out, normed_out
        )
        for r, rows_n in zip(both, normed):
            for row, out in ((pages + 1, own_out), (pages + 2, away_out)):
                slot = plan[row, r]

                @pl.when(slot >= 0)
                def _():
                    out[jnp.clip(slot, 0, CAP - 1)] = rows_n

        return carry

    lax.fori_loop(0, plan[pages + 4, 0], step, 0)


def own_kernel(plan, key_pool, value_pool, heads_q, heads_r, state_in, normed_in, own_in,
               state_out, normed_out, own_out):
    pages = plan.shape[0] - 5
    state_out[...] = state_in[...]
    normed_out[...] = normed_in[...]
    own_out[...] = own_in[...]

    def step(pair, carry):
        both, normed = attend_pair(
            plan, pair, key_pool, value_pool, heads_q, heads_r, state_out, normed_out
        )
        for r, rows_n in zip(both, normed):
            slot = plan[pages + 1, r]

            @pl.when(slot >= 0)
            def _():
                own_out[jnp.clip(slot, 0, CAP - 1)] = rows_n

        return carry

    lax.fori_loop(plan[pages + 4, 0], plan[pages + 4, 1], step, 0)


def rest_kernel(plan, key_pool, value_pool, heads_q, heads_r, state_in, normed_in, *rest):
    state_out, normed_out = rest[-2:]
    pages = plan.shape[0] - 5
    state_out[...] = state_in[...]
    normed_out[...] = normed_in[...]

    def step(pair, carry):
        attend_pair(plan, pair, key_pool, value_pool, heads_q, heads_r, state_out, normed_out)
        return carry

    lax.fori_loop(plan[pages + 4, 1], state_out.shape[0] // 2, step, 0)


def attend_shapes(rows, heads):
    packed = jax.ShapeDtypeStruct((CAP, heads, HEAD_DIM), BF16)
    return (
        jax.ShapeDtypeStruct((rows, heads, HEAD_DIM), F32),
        jax.ShapeDtypeStruct((rows, heads, HEAD_DIM), BF16),
        packed,
        packed,
    )


def attended(kernel, outs, cost, plan, key_pool, value_pool, heads_q, heads_r, *before):
    rows = plan.shape[1]
    heads = heads_q.shape[0] // rows
    return pl.pallas_call(
        kernel,
        out_shape=attend_shapes(rows, heads)[:outs],
        in_specs=[SMEM] + [VMEM] * (4 + len(before)),
        out_specs=(VMEM,) * outs,
        compiler_params=pltpu.CompilerParams(vmem_limit_bytes=8 << 20),
        cost_estimate=pl.CostEstimate(flops=cost, bytes_accessed=cost >> 4, transcendentals=0),
    )(plan, key_pool, value_pool, heads_q, heads_r, *before)


def expert_rows(rows, w_gate, w_up, w_down, split, flat, back):
    block, heads, _ = rows.shape
    split[...] = rows[...].astype(F32).reshape(block * heads, HEAD_DIM)
    for h in range(heads):
        cols = slice(h * HEAD_DIM, (h + 1) * HEAD_DIM)
        flat[:, cols] = split[pl.ds(h, block, stride=heads), :].astype(BF16)
    gate = jnp.dot(flat[...], w_gate[...], preferred_element_type=F32)
    up = jnp.dot(flat[...], w_up[...], preferred_element_type=F32)
    hidden = (gate / (1.0 + jnp.exp(-gate)) * up).astype(BF16)
    wide = 4
    for first in range(0, heads, wide):
        cols = slice(first * HEAD_DIM, (first + wide) * HEAD_DIM)
        part = jnp.dot(hidden, w_down[:, cols], preferred_element_type=F32)
        for h in range(wide):
            back[pl.ds(first + h, block, stride=heads), :] = part[
                :, h * HEAD_DIM:(h + 1) * HEAD_DIM
            ]


def expert_kernel(rows, w_gate, w_up, w_down, *rest):
    sums, split, flat, back = rest[-4:]
    expert_rows(rows, w_gate, w_up, w_down, split, flat, back)
    sums[...] = back[...].reshape(sums.shape).astype(sums.dtype)


def expert_parts(rows, w_gate, w_up, w_down, dtype, *after):
    total, heads, _ = rows.shape
    block = 8 * CAP
    if total % block:
        block = CAP
    spec = pl.BlockSpec((block, heads, HEAD_DIM), lambda i: (i, 0, 0))

    def fixed(array):
        return pl.BlockSpec(array.shape, lambda i: (0, 0))

    return pl.pallas_call(
        expert_kernel,
        grid=(total // block,),
        out_shape=jax.ShapeDtypeStruct(rows.shape, dtype),
        in_specs=[spec, fixed(w_gate), fixed(w_up), fixed(w_down)] + [ANY] * len(after),
        out_specs=spec,
        scratch_shapes=[
            pltpu.VMEM((block * heads, HEAD_DIM), F32),
            pltpu.VMEM((block, heads * HEAD_DIM), BF16),
            pltpu.VMEM((block * heads, HEAD_DIM), F32),
        ],
        compiler_params=pltpu.CompilerParams(vmem_limit_bytes=24 << 20),
        cost_estimate=pl.CostEstimate(
            flops=200_000_000, bytes_accessed=4 << 20, transcendentals=5120
        ),
    )(rows, w_gate, w_up, w_down, *after)


def join_kernel(own, away, *rest):
    both = rest[-1]
    both[:CAP] = own[...]
    both[CAP:] = away[...]


def joined(own, away, *after):
    return pl.pallas_call(
        join_kernel,
        out_shape=jax.ShapeDtypeStruct((2 * CAP,) + own.shape[1:], BF16),
        in_specs=[VMEM, VMEM] + [ANY] * len(after),
        out_specs=VMEM,
        compiler_params=pltpu.CompilerParams(vmem_limit_bytes=4 << 20),
    )(own, away, *after)


def hold_kernel(array, after, copy):
    copy[...] = array[...]


def held_back(array, after):
    return pl.pallas_call(
        hold_kernel,
        out_shape=jax.ShapeDtypeStruct(array.shape, array.dtype),
        in_specs=[VMEM, ANY],
        out_specs=VMEM,
        compiler_params=pltpu.CompilerParams(vmem_limit_bytes=4 << 20),
    )(array, after)


def gather_kernel(count, *refs):
    blocks, rows = refs[:count], refs[-1]
    size = blocks[0].shape[0]
    for i, block in enumerate(blocks):
        rows[i * size:(i + 1) * size] = block[...]


def gathered(blocks, *after):
    size, heads, depth = blocks[0].shape
    return pl.pallas_call(
        functools.partial(gather_kernel, len(blocks)),
        out_shape=jax.ShapeDtypeStruct((size * len(blocks), heads, depth), BF16),
        in_specs=[VMEM] * len(blocks) + [ANY] * len(after),
        out_specs=VMEM,
        compiler_params=pltpu.CompilerParams(vmem_limit_bytes=24 << 20),
    )(*blocks, *after)


def pair_sum_kernel(count, kept, received, *rest):
    parts = rest[-2 * count:]
    for i in range(count):
        for side in range(2):
            at = slice((2 * i + side) * CAP, (2 * i + side + 1) * CAP)
            parts[side * count + i][...] = (kept[at] + received[at].astype(F32)).astype(BF16)


def pair_sums(kept, received, *after):
    count = kept.shape[0] // (2 * CAP)
    part = jax.ShapeDtypeStruct((CAP,) + kept.shape[1:], BF16)
    parts = pl.pallas_call(
        functools.partial(pair_sum_kernel, count),
        out_shape=(part,) * (2 * count),
        in_specs=[VMEM, VMEM] + [ANY] * len(after),
        out_specs=(VMEM,) * (2 * count),
        compiler_params=pltpu.CompilerParams(vmem_limit_bytes=24 << 20),
    )(kept, received, *after)
    return parts[:count], parts[count:]


def finish_kernel(count, plan, mine, weights, state, away, *rest):
    owns, rest = rest[:count], rest[count:]
    arrived, (mixed, moved_keys, moved_values, rows_split, sems) = rest[:-5], rest[-5:]
    moves = moved_keys.shape[0]
    targets = [moved.at[m] for moved in (moved_keys, moved_values) for m in range(moves)]
    copies = [
        pltpu.make_async_copy(arrived[group].at[place], target, sems.at[i])
        for i, ((group, place), target) in enumerate(zip(PLACES, targets))
    ]
    for copy in copies:
        copy.start()
    rows, heads, _ = state.shape
    pages = plan.shape[0] - 5
    expert = mine[0]
    for r in range(rows):
        total = state[r]
        for row, sums, number in ((pages + 1, owns, expert), (pages + 2, (away,), 1 - expert)):
            slot = plan[row, r]
            factor = jnp.where(slot >= 0, weights[number, r], 0.0)
            at = jnp.clip(slot, 0, CAP - 1)
            total = total + factor * sum(part[at].astype(F32) for part in sums)
        rows_split[r * heads:(r + 1) * heads, :] = total
    for h in range(heads):
        mixed[:, h * HEAD_DIM:(h + 1) * HEAD_DIM] = rows_split[
            pl.ds(h, rows, stride=heads), :
        ].astype(BF16)
    for copy in copies:
        copy.wait()


def finished(plan, mine, weights, state, away, owns, arrived):
    rows, heads, _ = state.shape
    moved = jax.ShapeDtypeStruct((len(PLACES) // 2,) + arrived[0].shape[1:], BF16)
    return pl.pallas_call(
        functools.partial(finish_kernel, len(owns)),
        out_shape=(
            jax.ShapeDtypeStruct((rows, heads * HEAD_DIM), BF16),
            moved,
            moved,
        ),
        in_specs=[SMEM] * 3 + [VMEM] * (2 + len(owns)) + [ANY] * len(arrived),
        out_specs=(VMEM, HBM, HBM),
        scratch_shapes=[
            pltpu.VMEM((rows * heads, HEAD_DIM), F32),
            pltpu.SemaphoreType.DMA((len(PLACES),)),
        ],
        compiler_params=pltpu.CompilerParams(vmem_limit_bytes=8 << 20),
    )(plan, mine, weights, state, away, *owns, *arrived)


def gate_weights(normed, router_weight, chosen):
    rows, heads, _ = normed.shape
    router = router_weight.reshape(heads, HEAD_DIM, -1)
    logits = jnp.einsum("rhd,hde->re", normed, router, preferred_element_type=F32)
    numbers = jnp.arange(logits.shape[1], dtype=jnp.int32)[None, :]
    first = chosen[:, 0:1]
    second = chosen[:, 1:2]
    first_logit = jnp.sum(jnp.where(numbers == first, logits, 0.0), axis=1, keepdims=True)
    second_logit = jnp.sum(jnp.where(numbers == second, logits, 0.0), axis=1, keepdims=True)
    first_weight = 1.0 / (1.0 + jnp.exp(second_logit - first_logit))
    second_weight = 1.0 / (1.0 + jnp.exp(first_logit - second_logit))
    experts = jnp.arange(EXP_ON, dtype=jnp.int32)[None, :]
    weights = jnp.where(first == experts, first_weight, 0.0) + jnp.where(
        second == experts, second_weight, 0.0
    )
    return weights.T


def body(
    queries,
    residual,
    new_keys,
    new_values,
    key_pool,
    value_pool,
    page_table,
    lengths,
    migrate,
    chosen,
    router_weight,
    w_gate,
    w_up,
    w_down,
):
    length = lax.axis_size("attn")
    swap = length // 2
    masks = list(range(2, swap, 2))
    mine = (lax.axis_index("attn") // (length // EXP_ON)).astype(jnp.int32).reshape(1)
    along = [(i, (i + 1) % length) for i in range(length)]
    plan, keys, values, heads_q, heads_r, *leave = staged(
        page_table, lengths, migrate, chosen, mine, queries, residual, new_keys, new_values,
        key_pool, value_pool,
    )
    arrived = [None] * len(leave)
    arrived[0] = lax.ppermute(leave[0], "attn", along)
    arrived[1] = lax.ppermute(leave[1], "attn", along)
    held = (plan, keys, values, heads_q, heads_r)
    state, normed, own, away = attended(away_kernel, 4, COST, *held)
    swapped = exchanged(away, swap)
    state, normed, own = attended(own_kernel, 3, COST, *held, state, normed, own)
    rows_here = joined(own, swapped, arrived[0])
    blocks = [rows_here] + [exchanged(rows_here, mask) for mask in masks]
    state, normed = attended(rest_kernel, 2, COST, *held, state, normed, rows_here)
    mine_rows = gathered(blocks, state)
    weights = gate_weights(normed, router_weight, chosen)
    other_rows = exchanged(mine_rows, 1)
    kept = expert_parts(mine_rows, w_gate, w_up, w_down, F32)
    given = expert_parts(other_rows, w_gate, w_up, w_down, BF16, kept, arrived[1])
    own_parts, away_parts = pair_sums(kept, exchanged(given, 1))
    back = away_parts[0].astype(F32)
    for part, mask in zip(away_parts[1:], masks):
        back = back + exchanged(part, mask).astype(F32)
    own_sums = [own_parts[0]]
    own_sums += [exchanged(part, mask) for part, mask in zip(own_parts[1:], masks)]
    away_sums = exchanged(back.astype(BF16), swap)
    mixed, moved_keys, moved_values = finished(
        plan, mine, weights, state, away_sums, own_sums, arrived
    )
    return (mixed, moved_keys, moved_values)


def solution(mesh):
    placed = (
        P(("groups", "attn"), None),
        P(("groups", "attn"), None),
        P(("groups", "attn"), None),
        P(("groups", "attn"), None),
        P(("groups", "attn"), None, None),
        P(("groups", "attn"), None, None),
        P(("groups", "attn"), None),
        P(("groups", "attn")),
        P(("groups", "attn")),
        P(("groups", "attn"), None),
        P(),
        P(None, "attn"),
        P(None, "attn"),
        P("attn", None),
    )
    return jax.shard_map(
        body,
        mesh=mesh,
        in_specs=placed,
        out_specs=(
            P(("groups", "attn"), None),
            P(("groups", "attn"), None, None),
            P(("groups", "attn"), None, None),
        ),
        check_vma=False,
    )
```

```python
import functools
import math

import jax
import jax.numpy as jnp
from jax import lax
from jax.experimental import pallas as pl
from jax.experimental.pallas import tpu as pltpu
from jax.sharding import PartitionSpec as P

HEAD_DIM = 128
CAP = 5
EXP_ON = 2
F32 = jnp.float32
BF16 = jnp.bfloat16

SMEM = pl.BlockSpec(memory_space=pltpu.SMEM)
VMEM = pl.BlockSpec(memory_space=pltpu.VMEM)
ANY = pl.BlockSpec(memory_space=pl.ANY)
HBM = pl.BlockSpec(memory_space=pltpu.HBM)


def in_hbm(array):
    return pltpu.with_memory_space_constraint(array, pltpu.HBM)


def exchanged(array, mask):
    length = lax.axis_size("attn")
    return lax.ppermute(array, "attn", [(i, i ^ mask) for i in range(length)])


def stage_kernel(table_at, lengths_at, migrate_at, chosen_at, mine, queries_at, residual_at,
                 new_keys_at, new_values_at, key_pool_at, value_pool_at,
                 plan, key_pool, value_pool, heads_q, heads_r, *rest):
    moved, scratch = rest[:len(GROUPS)], rest[len(GROUPS):]
    (table, lengths, migrate, chosen, queries, residual, new_keys, new_values,
     fresh, small_sems, row_sems, pool_sems) = scratch
    pages, rows = table.shape
    page = key_pool.shape[1]
    moves = migrate.shape[0]
    heads = heads_q.shape[0] // rows
    small = [
        pltpu.make_async_copy(source, target, small_sems.at[i])
        for i, (source, target) in enumerate(
            ((table_at, table), (lengths_at, lengths), (migrate_at, migrate), (chosen_at, chosen))
        )
    ]
    wide = [
        pltpu.make_async_copy(source, target, row_sems.at[i])
        for i, (source, target) in enumerate(
            ((queries_at, queries), (residual_at, residual),
             (new_keys_at, new_keys), (new_values_at, new_values))
        )
    ]
    pool = []
    cut = key_pool.shape[0] // POOL_CUTS
    for c in range(POOL_CUTS):
        part = pl.ds(c * cut, cut)
        for side, (source, target) in enumerate(
            ((key_pool_at, key_pool), (value_pool_at, value_pool))
        ):
            pool.append(
                pltpu.make_async_copy(source.at[part], target.at[part], pool_sems.at[side, c])
            )
    for copy in wide[:2] + small + wide[2:] + pool:
        copy.start()
    for copy, target, source in zip(wide[:2], (heads_q, heads_r), (queries, residual)):
        copy.wait()
        for h in range(heads):
            target[pl.ds(h, rows, stride=heads), :] = source[
                :, h * HEAD_DIM:(h + 1) * HEAD_DIM
            ].astype(F32)
    for copy in small:
        copy.wait()
    expert = mine[0]
    other = 1 - expert
    taken_own, taken_away = jnp.int32(0), jnp.int32(0)
    own_slots, away_slots = [], []
    for r in range(rows):
        for p in range(pages):
            plan[p, r] = table[p, r]
        plan[pages, r] = lengths[r]
        first, second = chosen[0, r], chosen[1, r]
        own = ((first == expert) | (second == expert)).astype(jnp.int32)
        away = ((first == other) | (second == other)).astype(jnp.int32)
        own_slots.append(jnp.where(own == 1, taken_own, -1))
        away_slots.append(jnp.where(away == 1, taken_away, -1))
        plan[pages + 1, r] = own_slots[r]
        plan[pages + 2, r] = away_slots[r]
        taken_own = taken_own + own
        taken_away = taken_away + away
    only_own = [
        jnp.where(own_slot >= 0, 1, 0) * jnp.where(away_slot >= 0, 0, 1)
        for own_slot, away_slot in zip(own_slots, away_slots)
    ]
    middle = taken_away
    behind = taken_away + sum(only_own)
    for bound, count in enumerate((taken_away, behind)):
        plan[pages + 4, bound] = (count + 1) // 2
    for r in range(rows):
        is_away = away_slots[r] >= 0
        is_own = only_own[r] == 1
        place = jnp.where(is_away, away_slots[r], jnp.where(is_own, middle, behind))
        plan[pages + 3, place] = jnp.int32(r)
        middle = middle + only_own[r]
        behind = behind + jnp.where(is_away | is_own, 0, 1)
    for copy, side in zip(wide[2:], (0, 1)):
        copy.wait()
        fresh[side] = (new_keys, new_values)[side][...].astype(F32)
    for copy in pool:
        copy.wait()
    inside = lax.broadcasted_iota(jnp.int32, (page, key_pool.shape[2]), 0)
    for r in range(rows):
        length = lengths[r]
        last = length // page
        number = table[last, r]
        here = inside == length - last * page
        for side, buffer in enumerate((key_pool, value_pool)):
            block = buffer[number].astype(F32)
            buffer[number] = jnp.where(here, fresh[side, r:r + 1, :], block).astype(BF16)
    for m in range(moves):
        request = migrate[m]
        length = lengths[request]
        for p in range(pages):
            number = table[p, request]
            kept = inside + p * page <= length
            for side, buffer in enumerate((key_pool, value_pool)):
                group, place = PLACES[side * moves + m]
                block = jnp.where(kept, buffer[number].astype(F32), 0.0)
                moved[group][place, p * page:(p + 1) * page, :] = block.astype(BF16)


POOL_CUTS = 3
GROUPS = ((0,), (1, 2, 3))
PLACES = [(g, group.index(i)) for i in range(sum(map(len, GROUPS)))
          for g, group in enumerate(GROUPS) if i in group]
COST = 1 << 20


def staged(page_table, lengths, migrate, chosen, mine, queries, residual, new_keys, new_values,
           key_pool, value_pool):
    rows, width = queries.shape
    heads = width // HEAD_DIM
    kv_width = new_keys.shape[1]
    moves = migrate.shape[0]
    pages = page_table.shape[1]
    moved = tuple(
        jax.ShapeDtypeStruct((len(group), pages * key_pool.shape[1], kv_width), BF16)
        for group in GROUPS
    )
    split = jax.ShapeDtypeStruct((rows * heads, HEAD_DIM), F32)
    return pl.pallas_call(
        stage_kernel,
        out_shape=(
            jax.ShapeDtypeStruct((pages + 5, rows), jnp.int32),
            jax.ShapeDtypeStruct(key_pool.shape, BF16),
            jax.ShapeDtypeStruct(value_pool.shape, BF16),
            split, split,
        ) + moved,
        in_specs=[HBM] * 4 + [SMEM] + [HBM] * 6,
        out_specs=(SMEM,) + (VMEM,) * (4 + len(moved)),
        scratch_shapes=[
            pltpu.SMEM((pages, rows), jnp.int32),
            pltpu.SMEM(lengths.shape, jnp.int32),
            pltpu.SMEM(migrate.shape, jnp.int32),
            pltpu.SMEM((2, rows), jnp.int32),
            pltpu.VMEM(queries.shape, BF16),
            pltpu.VMEM(queries.shape, BF16),
            pltpu.VMEM(new_keys.shape, BF16),
            pltpu.VMEM(new_keys.shape, BF16),
            pltpu.VMEM((2, rows, kv_width), F32),
            pltpu.SemaphoreType.DMA((4,)),
            pltpu.SemaphoreType.DMA((4,)),
            pltpu.SemaphoreType.DMA((2, POOL_CUTS)),
        ],
        compiler_params=pltpu.CompilerParams(vmem_limit_bytes=16 << 20),
        cost_estimate=pl.CostEstimate(flops=0, bytes_accessed=8 << 20, transcendentals=0),
    )(*[in_hbm(a) for a in (page_table.T, lengths, migrate, chosen.T)], mine,
      *[in_hbm(a) for a in (queries, residual, new_keys, new_values, key_pool, value_pool)])


def attend_pair(plan, pair, key_pool, value_pool, heads_q, heads_r, state_out, normed_out):
    page = key_pool.shape[1]
    kv_heads = key_pool.shape[2] // HEAD_DIM
    rows, heads, _ = state_out.shape
    group = heads // kv_heads
    pages = plan.shape[0] - 5
    positions = pages * page
    head_of = lax.broadcasted_iota(jnp.int32, (heads, HEAD_DIM), 0)
    at_of = lax.broadcasted_iota(jnp.int32, (heads, positions), 1)
    in_group = [(head_of >= g * group) & (head_of < (g + 1) * group) for g in range(kv_heads)]
    both = [plan[pages + 3, 2 * pair + i] for i in range(2)]
    starts = [pl.multiple_of(r * heads, 8) for r in both]
    numbers = [[plan[p, r] for p in range(pages)] for r in both]
    queries = [heads_q[pl.ds(start, heads), :] for start in starts]
    spread = [
        jnp.concatenate(
            [jnp.where(inside, query, 0.0).astype(BF16) for inside in in_group], axis=1
        )
        for query in queries
    ]
    scores = [
        lax.dot_general(
            rows_q, jnp.concatenate([key_pool[n] for n in number], axis=0),
            (((1,), (1,)), ((), ())), preferred_element_type=F32,
        ) * (1.0 / math.sqrt(HEAD_DIM))
        for rows_q, number in zip(spread, numbers)
    ]
    visible = [at_of <= plan[pages, r] for r in both]
    scores = [jnp.where(seen, score, -jnp.inf) for seen, score in zip(visible, scores)]
    highest = [jnp.max(score, axis=1, keepdims=True) for score in scores]
    exponent = [
        jnp.where(seen, jnp.exp(score - high), 0.0)
        for seen, score, high in zip(visible, scores, highest)
    ]
    sums = [jnp.sum(e, axis=1, keepdims=True) for e in exponent]
    probs = [(e / s).astype(BF16) for e, s in zip(exponent, sums)]
    mixed = [
        jnp.dot(
            prob, jnp.concatenate([value_pool[n] for n in number], axis=0),
            preferred_element_type=F32,
        )
        for prob, number in zip(probs, numbers)
    ]
    states = []
    for start, mix in zip(starts, mixed):
        attended = mix[:, :HEAD_DIM]
        for g in range(1, kv_heads):
            attended = jnp.where(in_group[g], mix[:, g * HEAD_DIM:(g + 1) * HEAD_DIM], attended)
        states.append(heads_r[pl.ds(start, heads), :] + attended.astype(BF16).astype(F32))
    squares = [
        jnp.sum(jnp.sum(state * state, axis=1, keepdims=True), axis=0, keepdims=True)
        for state in states
    ]
    normed = [
        (state * lax.rsqrt(square / (heads * HEAD_DIM) + 1e-05)).astype(BF16)
        for state, square in zip(states, squares)
    ]
    for r, state, rows_n in zip(both, states, normed):
        state_out[r] = state
        normed_out[r] = rows_n
    return both, normed


def away_kernel(plan, key_pool, value_pool, heads_q, heads_r,
                state_out, normed_out, own_out, away_out):
    pages = plan.shape[0] - 5
    own_out[...] = jnp.zeros_like(own_out)
    away_out[...] = jnp.zeros_like(away_out)

    def step(pair, carry):
        both, normed = attend_pair(
            plan, pair, key_pool, value_pool, heads_q, heads_r, state_out, normed_out
        )
        for r, rows_n in zip(both, normed):
            for row, out in ((pages + 1, own_out), (pages + 2, away_out)):
                slot = plan[row, r]

                @pl.when(slot >= 0)
                def _():
                    out[jnp.clip(slot, 0, CAP - 1)] = rows_n

        return carry

    lax.fori_loop(0, plan[pages + 4, 0], step, 0)


def own_kernel(plan, key_pool, value_pool, heads_q, heads_r, state_in, normed_in, own_in,
               state_out, normed_out, own_out):
    pages = plan.shape[0] - 5
    state_out[...] = state_in[...]
    normed_out[...] = normed_in[...]
    own_out[...] = own_in[...]

    def step(pair, carry):
        both, normed = attend_pair(
            plan, pair, key_pool, value_pool, heads_q, heads_r, state_out, normed_out
        )
        for r, rows_n in zip(both, normed):
            slot = plan[pages + 1, r]

            @pl.when(slot >= 0)
            def _():
                own_out[jnp.clip(slot, 0, CAP - 1)] = rows_n

        return carry

    lax.fori_loop(plan[pages + 4, 0], plan[pages + 4, 1], step, 0)


def rest_kernel(plan, key_pool, value_pool, heads_q, heads_r, state_in, normed_in, *rest):
    state_out, normed_out = rest[-2:]
    pages = plan.shape[0] - 5
    state_out[...] = state_in[...]
    normed_out[...] = normed_in[...]

    def step(pair, carry):
        attend_pair(plan, pair, key_pool, value_pool, heads_q, heads_r, state_out, normed_out)
        return carry

    lax.fori_loop(plan[pages + 4, 1], state_out.shape[0] // 2, step, 0)


def attend_shapes(rows, heads):
    packed = jax.ShapeDtypeStruct((CAP, heads, HEAD_DIM), BF16)
    return (
        jax.ShapeDtypeStruct((rows, heads, HEAD_DIM), F32),
        jax.ShapeDtypeStruct((rows, heads, HEAD_DIM), BF16),
        packed,
        packed,
    )


def attended(kernel, outs, cost, plan, key_pool, value_pool, heads_q, heads_r, *before):
    rows = plan.shape[1]
    heads = heads_q.shape[0] // rows
    return pl.pallas_call(
        kernel,
        out_shape=attend_shapes(rows, heads)[:outs],
        in_specs=[SMEM] + [VMEM] * (4 + len(before)),
        out_specs=(VMEM,) * outs,
        compiler_params=pltpu.CompilerParams(vmem_limit_bytes=8 << 20),
        cost_estimate=pl.CostEstimate(flops=cost, bytes_accessed=cost >> 4, transcendentals=0),
    )(plan, key_pool, value_pool, heads_q, heads_r, *before)


def expert_kernel(block, rows, *rest):
    weights, (sums, split, flat, back) = rest[:6], rest[-4:]
    total, heads, _ = rows.shape
    units = weights[0].shape[1]
    deep = 4 * HEAD_DIM
    wide = 4

    def step(i, carry):
        here = pl.ds(i * block, block)
        split[...] = rows[here].astype(F32).reshape(block * heads, HEAD_DIM)
        for h in range(heads):
            cols = slice(h * HEAD_DIM, (h + 1) * HEAD_DIM)
            flat[:, cols] = split[pl.ds(h, block, stride=heads), :].astype(BF16)
        both = jnp.zeros((block, 4 * units), F32)
        for first in range(0, heads * HEAD_DIM, deep):
            at = slice(first, first + deep)
            both = both + jnp.dot(
                flat[:, at], jnp.concatenate([w[at] for w in weights[:4]], axis=1),
                preferred_element_type=F32,
            )
        gate, up = both[:, :2 * units], both[:, 2 * units:]
        hidden = (gate / (1.0 + jnp.exp(-gate)) * up).astype(BF16)
        for first in range(0, heads, wide):
            cols = slice(first * HEAD_DIM, (first + wide) * HEAD_DIM)
            part = jnp.dot(
                hidden, jnp.concatenate([w[:, cols] for w in weights[4:6]], axis=0),
                preferred_element_type=F32,
            )
            for h in range(wide):
                back[pl.ds(first + h, block, stride=heads), :] = part[
                    :, h * HEAD_DIM:(h + 1) * HEAD_DIM
                ]
        sums[here] = back[...].reshape(block, heads, HEAD_DIM).astype(BF16)
        return carry

    if total == block:
        step(0, 0)
    else:
        lax.fori_loop(0, total // block, step, 0)


def expert_parts(rows, weights, *after):
    total, heads, _ = rows.shape
    block = 8 * CAP
    if total % block:
        block = CAP
    return pl.pallas_call(
        functools.partial(expert_kernel, block),
        out_shape=jax.ShapeDtypeStruct(rows.shape, BF16),
        in_specs=[VMEM] * (1 + len(weights)) + [ANY] * len(after),
        out_specs=VMEM,
        scratch_shapes=[
            pltpu.VMEM((block * heads, HEAD_DIM), F32),
            pltpu.VMEM((block, heads * HEAD_DIM), BF16),
            pltpu.VMEM((block * heads, HEAD_DIM), F32),
        ],
        compiler_params=pltpu.CompilerParams(vmem_limit_bytes=8 << 20),
        cost_estimate=pl.CostEstimate(
            flops=400_000_000, bytes_accessed=10 << 20, transcendentals=10240
        ),
    )(rows, *weights, *after)


def join_kernel(own, away, *rest):
    both = rest[-1]
    both[:CAP] = own[...]
    both[CAP:] = away[...]


def joined(own, away, *after):
    return pl.pallas_call(
        join_kernel,
        out_shape=jax.ShapeDtypeStruct((2 * CAP,) + own.shape[1:], BF16),
        in_specs=[VMEM, VMEM] + [ANY] * len(after),
        out_specs=VMEM,
        compiler_params=pltpu.CompilerParams(vmem_limit_bytes=4 << 20),
    )(own, away, *after)


def hold_kernel(array, after, copy):
    copy[...] = array[...]


def held_back(array, after):
    return pl.pallas_call(
        hold_kernel,
        out_shape=jax.ShapeDtypeStruct(array.shape, array.dtype),
        in_specs=[VMEM, ANY],
        out_specs=VMEM,
        compiler_params=pltpu.CompilerParams(vmem_limit_bytes=4 << 20),
    )(array, after)


def gather_kernel(count, *refs):
    blocks, rows = refs[:count], refs[-1]
    size = blocks[0].shape[0]
    for i, block in enumerate(blocks):
        rows[i * size:(i + 1) * size] = block[...]


def gathered(blocks, *after):
    size, heads, depth = blocks[0].shape
    return pl.pallas_call(
        functools.partial(gather_kernel, len(blocks)),
        out_shape=jax.ShapeDtypeStruct((size * len(blocks), heads, depth), BF16),
        in_specs=[VMEM] * len(blocks) + [ANY] * len(after),
        out_specs=VMEM,
        compiler_params=pltpu.CompilerParams(vmem_limit_bytes=24 << 20),
    )(*blocks, *after)


def finish_kernel(count, plan, mine, weights, state, away, *rest):
    owns, rest = rest[:count], rest[count:]
    arrived, (mixed, moved_keys, moved_values, rows_split, sems) = rest[:-5], rest[-5:]
    moves = moved_keys.shape[0]
    targets = [moved.at[m] for moved in (moved_keys, moved_values) for m in range(moves)]
    copies = [
        pltpu.make_async_copy(arrived[group].at[place], target, sems.at[i])
        for i, ((group, place), target) in enumerate(zip(PLACES, targets))
    ]
    for copy in copies:
        copy.start()
    rows, heads, _ = state.shape
    pages = plan.shape[0] - 5
    expert = mine[0]
    for r in range(rows):
        total = state[r]
        for row, sums, number in ((pages + 1, owns, expert), (pages + 2, (away,), 1 - expert)):
            slot = plan[row, r]
            factor = jnp.where(slot >= 0, weights[number, r], 0.0)
            at = jnp.clip(slot, 0, CAP - 1)
            total = total + factor * sum(part[at].astype(F32) for part in sums)
        rows_split[r * heads:(r + 1) * heads, :] = total
    for h in range(heads):
        mixed[:, h * HEAD_DIM:(h + 1) * HEAD_DIM] = rows_split[
            pl.ds(h, rows, stride=heads), :
        ].astype(BF16)
    for copy in copies:
        copy.wait()


def finished(plan, mine, weights, state, away, owns, arrived):
    rows, heads, _ = state.shape
    moved = jax.ShapeDtypeStruct((len(PLACES) // 2,) + arrived[0].shape[1:], BF16)
    return pl.pallas_call(
        functools.partial(finish_kernel, len(owns)),
        out_shape=(
            jax.ShapeDtypeStruct((rows, heads * HEAD_DIM), BF16),
            moved,
            moved,
        ),
        in_specs=[SMEM] * 3 + [VMEM] * (2 + len(owns)) + [ANY] * len(arrived),
        out_specs=(VMEM, HBM, HBM),
        scratch_shapes=[
            pltpu.VMEM((rows * heads, HEAD_DIM), F32),
            pltpu.SemaphoreType.DMA((len(PLACES),)),
        ],
        compiler_params=pltpu.CompilerParams(vmem_limit_bytes=8 << 20),
    )(plan, mine, weights, state, away, *owns, *arrived)


def gate_weights(normed, router_weight, chosen):
    rows, heads, _ = normed.shape
    router = router_weight.reshape(heads, HEAD_DIM, -1)
    logits = jnp.einsum("rhd,hde->re", normed, router, preferred_element_type=F32)
    numbers = jnp.arange(logits.shape[1], dtype=jnp.int32)[None, :]
    first = chosen[:, 0:1]
    second = chosen[:, 1:2]
    first_logit = jnp.sum(jnp.where(numbers == first, logits, 0.0), axis=1, keepdims=True)
    second_logit = jnp.sum(jnp.where(numbers == second, logits, 0.0), axis=1, keepdims=True)
    first_weight = 1.0 / (1.0 + jnp.exp(second_logit - first_logit))
    second_weight = 1.0 / (1.0 + jnp.exp(first_logit - second_logit))
    experts = jnp.arange(EXP_ON, dtype=jnp.int32)[None, :]
    weights = jnp.where(first == experts, first_weight, 0.0) + jnp.where(
        second == experts, second_weight, 0.0
    )
    return weights.T


def body(
    queries,
    residual,
    new_keys,
    new_values,
    key_pool,
    value_pool,
    page_table,
    lengths,
    migrate,
    chosen,
    router_weight,
    w_gate,
    w_up,
    w_down,
):
    length = lax.axis_size("attn")
    swap = length // 2
    masks = list(range(2, swap, 2))
    mine = (lax.axis_index("attn") // (length // EXP_ON)).astype(jnp.int32).reshape(1)
    along = [(i, (i + 1) % length) for i in range(length)]
    plan, keys, values, heads_q, heads_r, *leave = staged(
        page_table, lengths, migrate, chosen, mine, queries, residual, new_keys, new_values,
        key_pool, value_pool,
    )
    arrived = [None] * len(leave)
    arrived[0] = lax.ppermute(leave[0], "attn", along)
    arrived[1] = lax.ppermute(leave[1], "attn", along)
    held = (plan, keys, values, heads_q, heads_r)
    state, normed, own, away = attended(away_kernel, 4, COST, *held)
    swapped = exchanged(away, swap)
    state, normed, own = attended(own_kernel, 3, COST, *held, state, normed, own)
    rows_here = joined(own, swapped, arrived[0])
    others = [exchanged(w, 1) for w in (w_gate, w_up, w_down)]
    blocks = [rows_here] + [exchanged(rows_here, mask) for mask in masks]
    state, normed = attended(rest_kernel, 2, COST, *held, state, normed, rows_here, *others)
    mine_rows = gathered(blocks, state)
    weights = gate_weights(normed, router_weight, chosen)
    sums = expert_parts(
        mine_rows, [w for pair in zip((w_gate, w_up, w_down), others) for w in pair]
    )
    parts = [sums[i * CAP:(i + 1) * CAP] for i in range(2 * len(blocks))]
    own_parts, away_parts = parts[0::2], parts[1::2]
    back = away_parts[0].astype(F32)
    for part, mask in zip(away_parts[1:], masks):
        back = back + exchanged(part, mask).astype(F32)
    own_sums = [own_parts[0]]
    own_sums += [exchanged(part, mask) for part, mask in zip(own_parts[1:], masks)]
    away_sums = exchanged(back.astype(BF16), swap)
    mixed, moved_keys, moved_values = finished(
        plan, mine, weights, state, away_sums, own_sums, arrived
    )
    return (mixed, moved_keys, moved_values)


def solution(mesh):
    placed = (
        P(("groups", "attn"), None),
        P(("groups", "attn"), None),
        P(("groups", "attn"), None),
        P(("groups", "attn"), None),
        P(("groups", "attn"), None, None),
        P(("groups", "attn"), None, None),
        P(("groups", "attn"), None),
        P(("groups", "attn")),
        P(("groups", "attn")),
        P(("groups", "attn"), None),
        P(),
        P(None, "attn"),
        P(None, "attn"),
        P("attn", None),
    )
    return jax.shard_map(
        body,
        mesh=mesh,
        in_specs=placed,
        out_specs=(
            P(("groups", "attn"), None),
            P(("groups", "attn"), None, None),
            P(("groups", "attn"), None, None),
        ),
        check_vma=False,
    )
```

```python
import functools
import math

import jax
import jax.numpy as jnp
from jax import lax
from jax.experimental import pallas as pl
from jax.experimental.pallas import tpu as pltpu
from jax.sharding import PartitionSpec as P

HEAD_DIM = 128
CAP = 5
EXP_ON = 2
F32 = jnp.float32
BF16 = jnp.bfloat16

SMEM = pl.BlockSpec(memory_space=pltpu.SMEM)
VMEM = pl.BlockSpec(memory_space=pltpu.VMEM)
ANY = pl.BlockSpec(memory_space=pl.ANY)
HBM = pl.BlockSpec(memory_space=pltpu.HBM)


def in_hbm(array):
    return pltpu.with_memory_space_constraint(array, pltpu.HBM)


def exchanged(array, mask):
    length = lax.axis_size("attn")
    return lax.ppermute(array, "attn", [(i, i ^ mask) for i in range(length)])


def stage_kernel(table_at, lengths_at, migrate_at, chosen_at, mine, queries_at, residual_at,
                 new_keys_at, new_values_at, key_pool_at, value_pool_at,
                 plan, key_pool, value_pool, heads_q, heads_r, *rest):
    moved, scratch = rest[:len(GROUPS)], rest[len(GROUPS):]
    (table, lengths, migrate, chosen, queries, residual, new_keys, new_values,
     fresh, small_sems, row_sems, pool_sems) = scratch
    pages, rows = table.shape
    page = key_pool.shape[1]
    moves = migrate.shape[0]
    heads = heads_q.shape[0] // rows
    small = [
        pltpu.make_async_copy(source, target, small_sems.at[i])
        for i, (source, target) in enumerate(
            ((table_at, table), (lengths_at, lengths), (migrate_at, migrate), (chosen_at, chosen))
        )
    ]
    wide = [
        pltpu.make_async_copy(source, target, row_sems.at[i])
        for i, (source, target) in enumerate(
            ((queries_at, queries), (residual_at, residual),
             (new_keys_at, new_keys), (new_values_at, new_values))
        )
    ]
    pool = []
    cut = key_pool.shape[0] // POOL_CUTS
    for c in range(POOL_CUTS):
        part = pl.ds(c * cut, cut)
        for side, (source, target) in enumerate(
            ((key_pool_at, key_pool), (value_pool_at, value_pool))
        ):
            pool.append(
                pltpu.make_async_copy(source.at[part], target.at[part], pool_sems.at[side, c])
            )
    for copy in wide[:2] + small + wide[2:] + pool:
        copy.start()
    for copy, target, source in zip(wide[:2], (heads_q, heads_r), (queries, residual)):
        copy.wait()
        for h in range(heads):
            target[pl.ds(h, rows, stride=heads), :] = source[
                :, h * HEAD_DIM:(h + 1) * HEAD_DIM
            ].astype(F32)
    for copy in small:
        copy.wait()
    expert = mine[0]
    other = 1 - expert
    taken_own, taken_away = jnp.int32(0), jnp.int32(0)
    own_slots, away_slots = [], []
    for r in range(rows):
        for p in range(pages):
            plan[p, r] = table[p, r]
        plan[pages, r] = lengths[r]
        first, second = chosen[0, r], chosen[1, r]
        own = ((first == expert) | (second == expert)).astype(jnp.int32)
        away = ((first == other) | (second == other)).astype(jnp.int32)
        own_slots.append(jnp.where(own == 1, taken_own, -1))
        away_slots.append(jnp.where(away == 1, taken_away, -1))
        plan[pages + 1, r] = own_slots[r]
        plan[pages + 2, r] = away_slots[r]
        taken_own = taken_own + own
        taken_away = taken_away + away
    only_own = [
        jnp.where(own_slot >= 0, 1, 0) * jnp.where(away_slot >= 0, 0, 1)
        for own_slot, away_slot in zip(own_slots, away_slots)
    ]
    middle = taken_away
    behind = taken_away + sum(only_own)
    plan[pages + 4, 0] = behind
    for r in range(rows):
        is_away = away_slots[r] >= 0
        is_own = only_own[r] == 1
        place = jnp.where(is_away, away_slots[r], jnp.where(is_own, middle, behind))
        plan[pages + 3, place] = jnp.int32(r)
        middle = middle + only_own[r]
        behind = behind + jnp.where(is_away | is_own, 0, 1)
    for copy, side in zip(wide[2:], (0, 1)):
        copy.wait()
        fresh[side] = (new_keys, new_values)[side][...].astype(F32)
    for copy in pool:
        copy.wait()
    inside = lax.broadcasted_iota(jnp.int32, (page, key_pool.shape[2]), 0)
    for r in range(rows):
        length = lengths[r]
        last = length // page
        number = table[last, r]
        here = inside == length - last * page
        for side, buffer in enumerate((key_pool, value_pool)):
            block = buffer[number].astype(F32)
            buffer[number] = jnp.where(here, fresh[side, r:r + 1, :], block).astype(BF16)
    for m in range(moves):
        request = migrate[m]
        length = lengths[request]
        for p in range(pages):
            number = table[p, request]
            kept = inside + p * page <= length
            for side, buffer in enumerate((key_pool, value_pool)):
                group, place = PLACES[side * moves + m]
                block = jnp.where(kept, buffer[number].astype(F32), 0.0)
                moved[group][place, p * page:(p + 1) * page, :] = block.astype(BF16)


POOL_CUTS = 3
GROUPS = ((0,), (1, 2, 3))
PLACES = [(g, group.index(i)) for i in range(sum(map(len, GROUPS)))
          for g, group in enumerate(GROUPS) if i in group]
COST = 1 << 20


def staged(page_table, lengths, migrate, chosen, mine, queries, residual, new_keys, new_values,
           key_pool, value_pool):
    rows, width = queries.shape
    heads = width // HEAD_DIM
    kv_width = new_keys.shape[1]
    moves = migrate.shape[0]
    pages = page_table.shape[1]
    moved = tuple(
        jax.ShapeDtypeStruct((len(group), pages * key_pool.shape[1], kv_width), BF16)
        for group in GROUPS
    )
    split = jax.ShapeDtypeStruct((rows * heads, HEAD_DIM), F32)
    return pl.pallas_call(
        stage_kernel,
        out_shape=(
            jax.ShapeDtypeStruct((pages + 5, rows), jnp.int32),
            jax.ShapeDtypeStruct(key_pool.shape, BF16),
            jax.ShapeDtypeStruct(value_pool.shape, BF16),
            split, split,
        ) + moved,
        in_specs=[HBM] * 4 + [SMEM] + [HBM] * 6,
        out_specs=(SMEM,) + (VMEM,) * (4 + len(moved)),
        scratch_shapes=[
            pltpu.SMEM((pages, rows), jnp.int32),
            pltpu.SMEM(lengths.shape, jnp.int32),
            pltpu.SMEM(migrate.shape, jnp.int32),
            pltpu.SMEM((2, rows), jnp.int32),
            pltpu.VMEM(queries.shape, BF16),
            pltpu.VMEM(queries.shape, BF16),
            pltpu.VMEM(new_keys.shape, BF16),
            pltpu.VMEM(new_keys.shape, BF16),
            pltpu.VMEM((2, rows, kv_width), F32),
            pltpu.SemaphoreType.DMA((4,)),
            pltpu.SemaphoreType.DMA((4,)),
            pltpu.SemaphoreType.DMA((2, POOL_CUTS)),
        ],
        compiler_params=pltpu.CompilerParams(vmem_limit_bytes=16 << 20),
        cost_estimate=pl.CostEstimate(flops=0, bytes_accessed=8 << 20, transcendentals=0),
    )(*[in_hbm(a) for a in (page_table.T, lengths, migrate, chosen.T)], mine,
      *[in_hbm(a) for a in (queries, residual, new_keys, new_values, key_pool, value_pool)])


def attend_some(plan, places, key_pool, value_pool, heads_q, heads_r, state_out, normed_out):
    page = key_pool.shape[1]
    kv_heads = key_pool.shape[2] // HEAD_DIM
    rows, heads, _ = state_out.shape
    group = heads // kv_heads
    pages = plan.shape[0] - 5
    positions = pages * page
    head_of = lax.broadcasted_iota(jnp.int32, (heads, HEAD_DIM), 0)
    at_of = lax.broadcasted_iota(jnp.int32, (heads, positions), 1)
    in_group = [(head_of >= g * group) & (head_of < (g + 1) * group) for g in range(kv_heads)]
    some = [plan[pages + 3, place] for place in places]
    starts = [pl.multiple_of(r * heads, 8) for r in some]
    numbers = [[plan[p, r] for p in range(pages)] for r in some]
    queries = [heads_q[pl.ds(start, heads), :] for start in starts]
    spread = [
        jnp.concatenate(
            [jnp.where(inside, query, 0.0).astype(BF16) for inside in in_group], axis=1
        )
        for query in queries
    ]
    scores = [
        lax.dot_general(
            rows_q, jnp.concatenate([key_pool[n] for n in number], axis=0),
            (((1,), (1,)), ((), ())), preferred_element_type=F32,
        ) * (1.0 / math.sqrt(HEAD_DIM))
        for rows_q, number in zip(spread, numbers)
    ]
    visible = [at_of <= plan[pages, r] for r in some]
    scores = [jnp.where(seen, score, -jnp.inf) for seen, score in zip(visible, scores)]
    highest = [jnp.max(score, axis=1, keepdims=True) for score in scores]
    exponent = [
        jnp.where(seen, jnp.exp(score - high), 0.0)
        for seen, score, high in zip(visible, scores, highest)
    ]
    sums = [jnp.sum(e, axis=1, keepdims=True) for e in exponent]
    probs = [(e / s).astype(BF16) for e, s in zip(exponent, sums)]
    mixed = [
        jnp.dot(
            prob, jnp.concatenate([value_pool[n] for n in number], axis=0),
            preferred_element_type=F32,
        )
        for prob, number in zip(probs, numbers)
    ]
    states = []
    for start, mix in zip(starts, mixed):
        attended = mix[:, :HEAD_DIM]
        for g in range(1, kv_heads):
            attended = jnp.where(in_group[g], mix[:, g * HEAD_DIM:(g + 1) * HEAD_DIM], attended)
        states.append(heads_r[pl.ds(start, heads), :] + attended.astype(BF16).astype(F32))
    squares = [
        jnp.sum(jnp.sum(state * state, axis=1, keepdims=True), axis=0, keepdims=True)
        for state in states
    ]
    normed = [
        (state * lax.rsqrt(square / (heads * HEAD_DIM) + 1e-05)).astype(BF16)
        for state, square in zip(states, squares)
    ]
    for r, state, rows_n in zip(some, states, normed):
        state_out[r] = state
        normed_out[r] = rows_n
    return some, normed


def away_kernel(plan, key_pool, value_pool, heads_q, heads_r,
                state_out, normed_out, own_out, away_out):
    pages = plan.shape[0] - 5
    own_out[...] = jnp.zeros_like(own_out)
    away_out[...] = jnp.zeros_like(away_out)
    some, normed = attend_some(
        plan, range(CAP), key_pool, value_pool, heads_q, heads_r, state_out, normed_out
    )
    for r, rows_n in zip(some, normed):
        for row, out in ((pages + 1, own_out), (pages + 2, away_out)):
            slot = plan[row, r]

            @pl.when(slot >= 0)
            def _():
                out[jnp.clip(slot, 0, CAP - 1)] = rows_n


def own_kernel(plan, key_pool, value_pool, heads_q, heads_r, state_in, normed_in, own_in,
               state_out, normed_out, own_out):
    pages = plan.shape[0] - 5
    state_out[...] = state_in[...]
    normed_out[...] = normed_in[...]
    own_out[...] = own_in[...]
    some, normed = attend_some(
        plan, range(CAP, state_out.shape[0]), key_pool, value_pool, heads_q, heads_r, state_out, normed_out
    )
    for r, rows_n in zip(some, normed):
        slot = plan[pages + 1, r]

        @pl.when(slot >= 0)
        def _():
            own_out[jnp.clip(slot, 0, CAP - 1)] = rows_n


def attend_shapes(rows, heads):
    packed = jax.ShapeDtypeStruct((CAP, heads, HEAD_DIM), BF16)
    return (
        jax.ShapeDtypeStruct((rows, heads, HEAD_DIM), F32),
        jax.ShapeDtypeStruct((rows, heads, HEAD_DIM), BF16),
        packed,
        packed,
    )


def attended(kernel, outs, cost, plan, key_pool, value_pool, heads_q, heads_r, *before):
    rows = plan.shape[1]
    heads = heads_q.shape[0] // rows
    return pl.pallas_call(
        kernel,
        out_shape=attend_shapes(rows, heads)[:outs],
        in_specs=[SMEM] + [VMEM] * (4 + len(before)),
        out_specs=(VMEM,) * outs,
        compiler_params=pltpu.CompilerParams(vmem_limit_bytes=8 << 20),
        cost_estimate=pl.CostEstimate(flops=cost, bytes_accessed=cost >> 4, transcendentals=0),
    )(plan, key_pool, value_pool, heads_q, heads_r, *before)


def expert_kernel(block, rows, *rest):
    weights, (sums, split, flat, back) = rest[:6], rest[-4:]
    total, heads, _ = rows.shape
    units = weights[0].shape[1]
    deep = 4 * HEAD_DIM
    wide = 4

    def step(i, carry):
        here = pl.ds(i * block, block)
        split[...] = rows[here].astype(F32).reshape(block * heads, HEAD_DIM)
        for h in range(heads):
            cols = slice(h * HEAD_DIM, (h + 1) * HEAD_DIM)
            flat[:, cols] = split[pl.ds(h, block, stride=heads), :].astype(BF16)
        both = jnp.zeros((block, 4 * units), F32)
        for first in range(0, heads * HEAD_DIM, deep):
            at = slice(first, first + deep)
            both = both + jnp.dot(
                flat[:, at], jnp.concatenate([w[at] for w in weights[:4]], axis=1),
                preferred_element_type=F32,
            )
        gate, up = both[:, :2 * units], both[:, 2 * units:]
        hidden = (gate / (1.0 + jnp.exp(-gate)) * up).astype(BF16)
        for first in range(0, heads, wide):
            cols = slice(first * HEAD_DIM, (first + wide) * HEAD_DIM)
            part = jnp.dot(
                hidden, jnp.concatenate([w[:, cols] for w in weights[4:6]], axis=0),
                preferred_element_type=F32,
            )
            for h in range(wide):
                back[pl.ds(first + h, block, stride=heads), :] = part[
                    :, h * HEAD_DIM:(h + 1) * HEAD_DIM
                ]
        sums[here] = back[...].reshape(block, heads, HEAD_DIM).astype(BF16)
        return carry

    if total == block:
        step(0, 0)
    else:
        lax.fori_loop(0, total // block, step, 0)


def expert_parts(rows, weights, *after):
    total, heads, _ = rows.shape
    block = 8 * CAP
    if total % block:
        block = CAP
    return pl.pallas_call(
        functools.partial(expert_kernel, block),
        out_shape=jax.ShapeDtypeStruct(rows.shape, BF16),
        in_specs=[VMEM] * (1 + len(weights)) + [ANY] * len(after),
        out_specs=VMEM,
        scratch_shapes=[
            pltpu.VMEM((block * heads, HEAD_DIM), F32),
            pltpu.VMEM((block, heads * HEAD_DIM), BF16),
            pltpu.VMEM((block * heads, HEAD_DIM), F32),
        ],
        compiler_params=pltpu.CompilerParams(vmem_limit_bytes=8 << 20),
        cost_estimate=pl.CostEstimate(
            flops=400_000_000, bytes_accessed=10 << 20, transcendentals=10240
        ),
    )(rows, *weights, *after)


def join_kernel(own, away, *rest):
    both = rest[-1]
    both[:CAP] = own[...]
    both[CAP:] = away[...]


def joined(own, away, *after):
    return pl.pallas_call(
        join_kernel,
        out_shape=jax.ShapeDtypeStruct((2 * CAP,) + own.shape[1:], BF16),
        in_specs=[VMEM, VMEM] + [ANY] * len(after),
        out_specs=VMEM,
        compiler_params=pltpu.CompilerParams(vmem_limit_bytes=4 << 20),
    )(own, away, *after)


def hold_kernel(count, *refs):
    for array, copy in zip(refs[:count], refs[-count:]):
        copy[...] = array[...]


def held_back(arrays, *after):
    count = len(arrays)
    return pl.pallas_call(
        functools.partial(hold_kernel, count),
        out_shape=tuple(jax.ShapeDtypeStruct(a.shape, a.dtype) for a in arrays),
        in_specs=[VMEM] * count + [ANY] * len(after),
        out_specs=(VMEM,) * count,
        compiler_params=pltpu.CompilerParams(vmem_limit_bytes=24 << 20),
    )(*arrays, *after)


def gather_kernel(count, *refs):
    blocks, rows = refs[:count], refs[-1]
    size = blocks[0].shape[0]
    for i, block in enumerate(blocks):
        rows[i * size:(i + 1) * size] = block[...]


def gathered(blocks, *after):
    size, heads, depth = blocks[0].shape
    return pl.pallas_call(
        functools.partial(gather_kernel, len(blocks)),
        out_shape=jax.ShapeDtypeStruct((size * len(blocks), heads, depth), BF16),
        in_specs=[VMEM] * len(blocks) + [ANY] * len(after),
        out_specs=VMEM,
        compiler_params=pltpu.CompilerParams(vmem_limit_bytes=24 << 20),
    )(*blocks, *after)


def finish_kernel(count, plan, mine, weights, state, away, *rest):
    owns, rest = rest[:count], rest[count:]
    mixed, rows_split = rest[-2:]
    rows, heads, _ = state.shape
    pages = plan.shape[0] - 5
    expert = mine[0]
    for r in range(rows):
        total = state[r]
        for row, sums, number in ((pages + 1, owns, expert), (pages + 2, (away,), 1 - expert)):
            slot = plan[row, r]
            factor = jnp.where(slot >= 0, weights[number, r], 0.0)
            at = jnp.clip(slot, 0, CAP - 1)
            total = total + factor * sum(part[at].astype(F32) for part in sums)
        rows_split[r * heads:(r + 1) * heads, :] = total
    for h in range(heads):
        mixed[:, h * HEAD_DIM:(h + 1) * HEAD_DIM] = rows_split[
            pl.ds(h, rows, stride=heads), :
        ].astype(BF16)


def finished(plan, mine, weights, state, away, owns, *after):
    rows, heads, _ = state.shape
    return pl.pallas_call(
        functools.partial(finish_kernel, len(owns)),
        out_shape=jax.ShapeDtypeStruct((rows, heads * HEAD_DIM), BF16),
        in_specs=[SMEM] * 3 + [VMEM] * (2 + len(owns)) + [ANY] * len(after),
        out_specs=VMEM,
        scratch_shapes=[pltpu.VMEM((rows * heads, HEAD_DIM), F32)],
        compiler_params=pltpu.CompilerParams(vmem_limit_bytes=8 << 20),
    )(plan, mine, weights, state, away, *owns, *after)


def deliver_kernel(count, *refs):
    arrived, (moved_keys, moved_values, sems) = refs[:count], refs[-3:]
    moves = moved_keys.shape[0]
    targets = [moved.at[m] for moved in (moved_keys, moved_values) for m in range(moves)]
    copies = [
        pltpu.make_async_copy(arrived[group].at[place], target, sems.at[i])
        for i, ((group, place), target) in enumerate(zip(PLACES, targets))
    ]
    for copy in copies:
        copy.start()
    for copy in copies:
        copy.wait()


def delivered(arrived, *after):
    moved = jax.ShapeDtypeStruct((len(PLACES) // 2,) + arrived[0].shape[1:], BF16)
    return pl.pallas_call(
        functools.partial(deliver_kernel, len(arrived)),
        out_shape=(moved, moved),
        in_specs=[ANY] * (len(arrived) + len(after)),
        out_specs=(HBM, HBM),
        scratch_shapes=[pltpu.SemaphoreType.DMA((len(PLACES),))],
        compiler_params=pltpu.CompilerParams(vmem_limit_bytes=4 << 20),
    )(*arrived, *after)


def gate_weights(normed, router_weight, chosen):
    rows, heads, _ = normed.shape
    router = router_weight.reshape(heads, HEAD_DIM, -1)
    logits = jnp.einsum("rhd,hde->re", normed, router, preferred_element_type=F32)
    numbers = jnp.arange(logits.shape[1], dtype=jnp.int32)[None, :]
    first = chosen[:, 0:1]
    second = chosen[:, 1:2]
    first_logit = jnp.sum(jnp.where(numbers == first, logits, 0.0), axis=1, keepdims=True)
    second_logit = jnp.sum(jnp.where(numbers == second, logits, 0.0), axis=1, keepdims=True)
    first_weight = 1.0 / (1.0 + jnp.exp(second_logit - first_logit))
    second_weight = 1.0 / (1.0 + jnp.exp(first_logit - second_logit))
    experts = jnp.arange(EXP_ON, dtype=jnp.int32)[None, :]
    weights = jnp.where(first == experts, first_weight, 0.0) + jnp.where(
        second == experts, second_weight, 0.0
    )
    return weights.T


def body(
    queries,
    residual,
    new_keys,
    new_values,
    key_pool,
    value_pool,
    page_table,
    lengths,
    migrate,
    chosen,
    router_weight,
    w_gate,
    w_up,
    w_down,
):
    length = lax.axis_size("attn")
    swap = length // 2
    masks = list(range(2, swap, 2))
    mine = (lax.axis_index("attn") // (length // EXP_ON)).astype(jnp.int32).reshape(1)
    along = [(i, (i + 1) % length) for i in range(length)]
    plan, keys, values, heads_q, heads_r, *leave = staged(
        page_table, lengths, migrate, chosen, mine, queries, residual, new_keys, new_values,
        key_pool, value_pool,
    )
    arrived = [None] * len(leave)
    arrived[0] = lax.ppermute(leave[0], "attn", along)
    arrived[1] = lax.ppermute(leave[1], "attn", along)
    held = (plan, keys, values, heads_q, heads_r)
    state, normed, own, away = attended(away_kernel, 4, COST, *held)
    swapped = exchanged(away, swap)
    state, normed, own = attended(own_kernel, 3, COST, *held, state, normed, own)
    rows_here = joined(own, swapped, arrived[0])
    others = [exchanged(w, 1) for w in (w_gate, w_up, w_down)]
    blocks = [rows_here] + [exchanged(rows_here, mask) for mask in masks]
    normed, = held_back([normed], rows_here, *others)
    mine_rows = gathered(blocks, normed)
    weights = gate_weights(normed, router_weight, chosen)
    sums = expert_parts(
        mine_rows, [w for pair in zip((w_gate, w_up, w_down), others) for w in pair]
    )
    parts = [sums[i * CAP:(i + 1) * CAP] for i in range(2 * len(blocks))]
    own_parts, away_parts = parts[0::2], parts[1::2]
    back = away_parts[0].astype(F32)
    for part, mask in zip(away_parts[1:], masks):
        back = back + exchanged(part, mask).astype(F32)
    own_sums = [own_parts[0]]
    own_sums += [exchanged(part, mask) for part, mask in zip(own_parts[1:], masks)]
    away_sums = exchanged(back.astype(BF16), swap)
    moved_keys, moved_values = delivered(arrived, back)
    mixed = finished(plan, mine, weights, state, away_sums, own_sums, in_hbm(moved_keys))
    return (mixed, moved_keys, moved_values)


def solution(mesh):
    placed = (
        P(("groups", "attn"), None),
        P(("groups", "attn"), None),
        P(("groups", "attn"), None),
        P(("groups", "attn"), None),
        P(("groups", "attn"), None, None),
        P(("groups", "attn"), None, None),
        P(("groups", "attn"), None),
        P(("groups", "attn")),
        P(("groups", "attn")),
        P(("groups", "attn"), None),
        P(),
        P(None, "attn"),
        P(None, "attn"),
        P("attn", None),
    )
    return jax.shard_map(
        body,
        mesh=mesh,
        in_specs=placed,
        out_specs=(
            P(("groups", "attn"), None),
            P(("groups", "attn"), None, None),
            P(("groups", "attn"), None, None),
        ),
        check_vma=False,
    )
```

```python
import functools
import math

import jax
import jax.numpy as jnp
from jax import lax
from jax.experimental import pallas as pl
from jax.experimental.pallas import tpu as pltpu
from jax.sharding import PartitionSpec as P

HEAD_DIM = 128
CAP = 5
EXP_ON = 2
F32 = jnp.float32
BF16 = jnp.bfloat16

SMEM = pl.BlockSpec(memory_space=pltpu.SMEM)
VMEM = pl.BlockSpec(memory_space=pltpu.VMEM)
ANY = pl.BlockSpec(memory_space=pl.ANY)
HBM = pl.BlockSpec(memory_space=pltpu.HBM)


def in_hbm(array):
    return pltpu.with_memory_space_constraint(array, pltpu.HBM)


def exchanged(array, mask):
    length = lax.axis_size("attn")
    return lax.ppermute(array, "attn", [(i, i ^ mask) for i in range(length)])


def stage_kernel(table_at, lengths_at, migrate_at, chosen_at, mine, queries_at, residual_at,
                 new_keys_at, new_values_at, key_pool_at, value_pool_at,
                 plan, key_pool, value_pool, heads_q, heads_r, *rest):
    moved, scratch = rest[:len(GROUPS)], rest[len(GROUPS):]
    (table, lengths, migrate, chosen, queries, residual, new_keys, new_values,
     fresh, small_sems, row_sems, pool_sems) = scratch
    pages, rows = table.shape
    page = key_pool.shape[1]
    moves = migrate.shape[0]
    heads = heads_q.shape[0] // rows
    small = [
        pltpu.make_async_copy(source, target, small_sems.at[i])
        for i, (source, target) in enumerate(
            ((table_at, table), (lengths_at, lengths), (migrate_at, migrate), (chosen_at, chosen))
        )
    ]
    wide = [
        pltpu.make_async_copy(source, target, row_sems.at[i])
        for i, (source, target) in enumerate(
            ((queries_at, queries), (residual_at, residual),
             (new_keys_at, new_keys), (new_values_at, new_values))
        )
    ]
    pool = []
    cut = key_pool.shape[0] // POOL_CUTS
    for c in range(POOL_CUTS):
        part = pl.ds(c * cut, cut)
        for side, (source, target) in enumerate(
            ((key_pool_at, key_pool), (value_pool_at, value_pool))
        ):
            pool.append(
                pltpu.make_async_copy(source.at[part], target.at[part], pool_sems.at[side, c])
            )
    for copy in wide[:2] + small + wide[2:] + pool:
        copy.start()
    for copy, target, source in zip(wide[:2], (heads_q, heads_r), (queries, residual)):
        copy.wait()
        for h in range(heads):
            target[pl.ds(h, rows, stride=heads), :] = source[
                :, h * HEAD_DIM:(h + 1) * HEAD_DIM
            ].astype(F32)
    for copy in small:
        copy.wait()
    expert = mine[0]
    other = 1 - expert
    taken_own, taken_away = jnp.int32(0), jnp.int32(0)
    own_slots, away_slots = [], []
    for r in range(rows):
        for p in range(pages):
            plan[p, r] = table[p, r]
        plan[pages, r] = lengths[r]
        first, second = chosen[0, r], chosen[1, r]
        own = ((first == expert) | (second == expert)).astype(jnp.int32)
        away = ((first == other) | (second == other)).astype(jnp.int32)
        own_slots.append(jnp.where(own == 1, taken_own, -1))
        away_slots.append(jnp.where(away == 1, taken_away, -1))
        plan[pages + 1, r] = own_slots[r]
        plan[pages + 2, r] = away_slots[r]
        taken_own = taken_own + own
        taken_away = taken_away + away
    only_own = [
        jnp.where(own_slot >= 0, 1, 0) * jnp.where(away_slot >= 0, 0, 1)
        for own_slot, away_slot in zip(own_slots, away_slots)
    ]
    middle = taken_away
    behind = taken_away + sum(only_own)
    plan[pages + 4, 0] = behind
    for r in range(rows):
        is_away = away_slots[r] >= 0
        is_own = only_own[r] == 1
        place = jnp.where(is_away, away_slots[r], jnp.where(is_own, middle, behind))
        plan[pages + 3, place] = jnp.int32(r)
        middle = middle + only_own[r]
        behind = behind + jnp.where(is_away | is_own, 0, 1)
    for copy, side in zip(wide[2:], (0, 1)):
        copy.wait()
        fresh[side] = (new_keys, new_values)[side][...].astype(F32)
    for copy in pool:
        copy.wait()
    inside = lax.broadcasted_iota(jnp.int32, (page, key_pool.shape[2]), 0)
    for r in range(rows):
        length = lengths[r]
        last = length // page
        number = table[last, r]
        here = inside == length - last * page
        for side, buffer in enumerate((key_pool, value_pool)):
            block = buffer[number].astype(F32)
            buffer[number] = jnp.where(here, fresh[side, r:r + 1, :], block).astype(BF16)
    for m in range(moves):
        request = migrate[m]
        length = lengths[request]
        for p in range(pages):
            number = table[p, request]
            kept = inside + p * page <= length
            for side, buffer in enumerate((key_pool, value_pool)):
                group, place = PLACES[side * moves + m]
                block = jnp.where(kept, buffer[number].astype(F32), 0.0)
                moved[group][place, p * page:(p + 1) * page, :] = block.astype(BF16)


POOL_CUTS = 3
GROUPS = ((0,), (1, 2, 3))
PLACES = [(g, group.index(i)) for i in range(sum(map(len, GROUPS)))
          for g, group in enumerate(GROUPS) if i in group]
COST = 1 << 20


def staged(page_table, lengths, migrate, chosen, mine, queries, residual, new_keys, new_values,
           key_pool, value_pool):
    rows, width = queries.shape
    heads = width // HEAD_DIM
    kv_width = new_keys.shape[1]
    moves = migrate.shape[0]
    pages = page_table.shape[1]
    moved = tuple(
        jax.ShapeDtypeStruct((len(group), pages * key_pool.shape[1], kv_width), BF16)
        for group in GROUPS
    )
    split = jax.ShapeDtypeStruct((rows * heads, HEAD_DIM), F32)
    return pl.pallas_call(
        stage_kernel,
        out_shape=(
            jax.ShapeDtypeStruct((pages + 5, rows), jnp.int32),
            jax.ShapeDtypeStruct(key_pool.shape, BF16),
            jax.ShapeDtypeStruct(value_pool.shape, BF16),
            split, split,
        ) + moved,
        in_specs=[HBM] * 4 + [SMEM] + [HBM] * 6,
        out_specs=(SMEM,) + (VMEM,) * (4 + len(moved)),
        scratch_shapes=[
            pltpu.SMEM((pages, rows), jnp.int32),
            pltpu.SMEM(lengths.shape, jnp.int32),
            pltpu.SMEM(migrate.shape, jnp.int32),
            pltpu.SMEM((2, rows), jnp.int32),
            pltpu.VMEM(queries.shape, BF16),
            pltpu.VMEM(queries.shape, BF16),
            pltpu.VMEM(new_keys.shape, BF16),
            pltpu.VMEM(new_keys.shape, BF16),
            pltpu.VMEM((2, rows, kv_width), F32),
            pltpu.SemaphoreType.DMA((4,)),
            pltpu.SemaphoreType.DMA((4,)),
            pltpu.SemaphoreType.DMA((2, POOL_CUTS)),
        ],
        compiler_params=pltpu.CompilerParams(vmem_limit_bytes=16 << 20),
        cost_estimate=pl.CostEstimate(flops=0, bytes_accessed=8 << 20, transcendentals=0),
    )(*[in_hbm(a) for a in (page_table.T, lengths, migrate, chosen.T)], mine,
      *[in_hbm(a) for a in (queries, residual, new_keys, new_values, key_pool, value_pool)])


def attend_some(plan, places, key_pool, value_pool, heads_q, heads_r, state_out, normed_out):
    page = key_pool.shape[1]
    kv_heads = key_pool.shape[2] // HEAD_DIM
    rows, heads, _ = state_out.shape
    group = heads // kv_heads
    pages = plan.shape[0] - 5
    positions = pages * page
    head_of = lax.broadcasted_iota(jnp.int32, (heads, HEAD_DIM), 0)
    at_of = lax.broadcasted_iota(jnp.int32, (heads, positions), 1)
    in_group = [(head_of >= g * group) & (head_of < (g + 1) * group) for g in range(kv_heads)]
    some = [plan[pages + 3, place] for place in places]
    starts = [pl.multiple_of(r * heads, 8) for r in some]
    numbers = [[plan[p, r] for p in range(pages)] for r in some]
    queries = [heads_q[pl.ds(start, heads), :] for start in starts]
    spread = [
        jnp.concatenate(
            [jnp.where(inside, query, 0.0).astype(BF16) for inside in in_group], axis=1
        )
        for query in queries
    ]
    scores = [
        lax.dot_general(
            rows_q, jnp.concatenate([key_pool[n] for n in number], axis=0),
            (((1,), (1,)), ((), ())), preferred_element_type=F32,
        ) * (1.0 / math.sqrt(HEAD_DIM))
        for rows_q, number in zip(spread, numbers)
    ]
    visible = [at_of <= plan[pages, r] for r in some]
    scores = [jnp.where(seen, score, -jnp.inf) for seen, score in zip(visible, scores)]
    highest = [jnp.max(score, axis=1, keepdims=True) for score in scores]
    exponent = [
        jnp.where(seen, jnp.exp(score - high), 0.0)
        for seen, score, high in zip(visible, scores, highest)
    ]
    sums = [jnp.sum(e, axis=1, keepdims=True) for e in exponent]
    probs = [(e / s).astype(BF16) for e, s in zip(exponent, sums)]
    mixed = [
        jnp.dot(
            prob, jnp.concatenate([value_pool[n] for n in number], axis=0),
            preferred_element_type=F32,
        )
        for prob, number in zip(probs, numbers)
    ]
    states = []
    for start, mix in zip(starts, mixed):
        attended = mix[:, :HEAD_DIM]
        for g in range(1, kv_heads):
            attended = jnp.where(in_group[g], mix[:, g * HEAD_DIM:(g + 1) * HEAD_DIM], attended)
        states.append(heads_r[pl.ds(start, heads), :] + attended.astype(BF16).astype(F32))
    squares = [
        jnp.sum(jnp.sum(state * state, axis=1, keepdims=True), axis=0, keepdims=True)
        for state in states
    ]
    normed = [
        (state * lax.rsqrt(square / (heads * HEAD_DIM) + 1e-05)).astype(BF16)
        for state, square in zip(states, squares)
    ]
    for r, state, rows_n in zip(some, states, normed):
        state_out[r] = state
        normed_out[r] = rows_n
    return some, normed


def away_kernel(plan, key_pool, value_pool, heads_q, heads_r,
                state_out, normed_out, own_out, away_out):
    pages = plan.shape[0] - 5
    own_out[...] = jnp.zeros_like(own_out)
    away_out[...] = jnp.zeros_like(away_out)
    some, normed = attend_some(
        plan, range(CAP), key_pool, value_pool, heads_q, heads_r, state_out, normed_out
    )
    for r, rows_n in zip(some, normed):
        for row, out in ((pages + 1, own_out), (pages + 2, away_out)):
            slot = plan[row, r]

            @pl.when(slot >= 0)
            def _():
                out[jnp.clip(slot, 0, CAP - 1)] = rows_n


def own_kernel(plan, key_pool, value_pool, heads_q, heads_r, state_in, normed_in, own_in,
               state_out, normed_out, own_out):
    pages = plan.shape[0] - 5
    state_out[...] = state_in[...]
    normed_out[...] = normed_in[...]
    own_out[...] = own_in[...]
    some, normed = attend_some(
        plan, range(CAP, state_out.shape[0]), key_pool, value_pool, heads_q, heads_r, state_out, normed_out
    )
    for r, rows_n in zip(some, normed):
        slot = plan[pages + 1, r]

        @pl.when(slot >= 0)
        def _():
            own_out[jnp.clip(slot, 0, CAP - 1)] = rows_n


def attend_shapes(rows, heads):
    packed = jax.ShapeDtypeStruct((CAP, heads, HEAD_DIM), BF16)
    return (
        jax.ShapeDtypeStruct((rows, heads, HEAD_DIM), F32),
        jax.ShapeDtypeStruct((rows, heads, HEAD_DIM), BF16),
        packed,
        packed,
    )


def attended(kernel, outs, cost, plan, key_pool, value_pool, heads_q, heads_r, *before):
    rows = plan.shape[1]
    heads = heads_q.shape[0] // rows
    return pl.pallas_call(
        kernel,
        out_shape=attend_shapes(rows, heads)[:outs],
        in_specs=[SMEM] + [VMEM] * (4 + len(before)),
        out_specs=(VMEM,) * outs,
        compiler_params=pltpu.CompilerParams(vmem_limit_bytes=8 << 20),
        cost_estimate=pl.CostEstimate(flops=cost, bytes_accessed=cost >> 4, transcendentals=0),
    )(plan, key_pool, value_pool, heads_q, heads_r, *before)


def expert_kernel(block, rows, *rest):
    weights, (sums, split, flat, back) = rest[:6], rest[-4:]
    total, heads, _ = rows.shape
    units = weights[0].shape[1]
    deep = 4 * HEAD_DIM
    wide = 4

    def step(i, carry):
        here = pl.ds(i * block, block)
        split[...] = rows[here].astype(F32).reshape(block * heads, HEAD_DIM)
        for h in range(heads):
            cols = slice(h * HEAD_DIM, (h + 1) * HEAD_DIM)
            flat[:, cols] = split[pl.ds(h, block, stride=heads), :].astype(BF16)
        both = jnp.zeros((block, 4 * units), F32)
        for first in range(0, heads * HEAD_DIM, deep):
            at = slice(first, first + deep)
            both = both + jnp.dot(
                flat[:, at], jnp.concatenate([w[at] for w in weights[:4]], axis=1),
                preferred_element_type=F32,
            )
        gate, up = both[:, :2 * units], both[:, 2 * units:]
        hidden = (gate / (1.0 + jnp.exp(-gate)) * up).astype(BF16)
        for first in range(0, heads, wide):
            cols = slice(first * HEAD_DIM, (first + wide) * HEAD_DIM)
            part = jnp.dot(
                hidden, jnp.concatenate([w[:, cols] for w in weights[4:6]], axis=0),
                preferred_element_type=F32,
            )
            for h in range(wide):
                back[pl.ds(first + h, block, stride=heads), :] = part[
                    :, h * HEAD_DIM:(h + 1) * HEAD_DIM
                ]
        sums[here] = back[...].reshape(block, heads, HEAD_DIM).astype(BF16)
        return carry

    if total == block:
        step(0, 0)
    else:
        lax.fori_loop(0, total // block, step, 0)


def expert_parts(rows, weights, *after):
    total, heads, _ = rows.shape
    block = 8 * CAP
    if total % block:
        block = CAP
    return pl.pallas_call(
        functools.partial(expert_kernel, block),
        out_shape=jax.ShapeDtypeStruct(rows.shape, BF16),
        in_specs=[VMEM] * (1 + len(weights)) + [ANY] * len(after),
        out_specs=VMEM,
        scratch_shapes=[
            pltpu.VMEM((block * heads, HEAD_DIM), F32),
            pltpu.VMEM((block, heads * HEAD_DIM), BF16),
            pltpu.VMEM((block * heads, HEAD_DIM), F32),
        ],
        compiler_params=pltpu.CompilerParams(vmem_limit_bytes=8 << 20),
        cost_estimate=pl.CostEstimate(
            flops=400_000_000, bytes_accessed=10 << 20, transcendentals=10240
        ),
    )(rows, *weights, *after)


def join_kernel(own, away, *rest):
    both = rest[-1]
    both[:CAP] = own[...]
    both[CAP:] = away[...]


def joined(own, away, *after):
    return pl.pallas_call(
        join_kernel,
        out_shape=jax.ShapeDtypeStruct((2 * CAP,) + own.shape[1:], BF16),
        in_specs=[VMEM, VMEM] + [ANY] * len(after),
        out_specs=VMEM,
        compiler_params=pltpu.CompilerParams(vmem_limit_bytes=4 << 20),
    )(own, away, *after)


def hold_kernel(count, *refs):
    for array, copy in zip(refs[:count], refs[-count:]):
        copy[...] = array[...]


def held_back(arrays, *after):
    count = len(arrays)
    return pl.pallas_call(
        functools.partial(hold_kernel, count),
        out_shape=tuple(jax.ShapeDtypeStruct(a.shape, a.dtype) for a in arrays),
        in_specs=[VMEM] * count + [ANY] * len(after),
        out_specs=(VMEM,) * count,
        compiler_params=pltpu.CompilerParams(vmem_limit_bytes=24 << 20),
    )(*arrays, *after)


def gather_kernel(count, *refs):
    blocks, rows = refs[:count], refs[-1]
    size = blocks[0].shape[0]
    for i, block in enumerate(blocks):
        rows[i * size:(i + 1) * size] = block[...]


def gathered(blocks, *after):
    size, heads, depth = blocks[0].shape
    return pl.pallas_call(
        functools.partial(gather_kernel, len(blocks)),
        out_shape=jax.ShapeDtypeStruct((size * len(blocks), heads, depth), BF16),
        in_specs=[VMEM] * len(blocks) + [ANY] * len(after),
        out_specs=VMEM,
        compiler_params=pltpu.CompilerParams(vmem_limit_bytes=24 << 20),
    )(*blocks, *after)


def finish_kernel(count, plan, mine, weights, state, away, *rest):
    owns, rest = rest[:count], rest[count:]
    mixed, rows_split = rest[-2:]
    rows, heads, _ = state.shape
    pages = plan.shape[0] - 5
    expert = mine[0]
    for r in range(rows):
        total = state[r]
        for row, sums, number in ((pages + 1, owns, expert), (pages + 2, (away,), 1 - expert)):
            slot = plan[row, r]
            factor = jnp.where(slot >= 0, weights[number, r], 0.0)
            at = jnp.clip(slot, 0, CAP - 1)
            total = total + factor * sum(part[at].astype(F32) for part in sums)
        rows_split[r * heads:(r + 1) * heads, :] = total
    for h in range(heads):
        mixed[:, h * HEAD_DIM:(h + 1) * HEAD_DIM] = rows_split[
            pl.ds(h, rows, stride=heads), :
        ].astype(BF16)


def finished(plan, mine, weights, state, away, owns, *after):
    rows, heads, _ = state.shape
    return pl.pallas_call(
        functools.partial(finish_kernel, len(owns)),
        out_shape=jax.ShapeDtypeStruct((rows, heads * HEAD_DIM), BF16),
        in_specs=[SMEM] * 3 + [VMEM] * (2 + len(owns)) + [ANY] * len(after),
        out_specs=VMEM,
        scratch_shapes=[pltpu.VMEM((rows * heads, HEAD_DIM), F32)],
        compiler_params=pltpu.CompilerParams(vmem_limit_bytes=8 << 20),
    )(plan, mine, weights, state, away, *owns, *after)


def deliver_kernel(count, *refs):
    arrived, (moved_keys, moved_values, sems) = refs[:count], refs[-3:]
    moves = moved_keys.shape[0]
    targets = [moved.at[m] for moved in (moved_keys, moved_values) for m in range(moves)]
    copies = [
        pltpu.make_async_copy(arrived[group].at[place], target, sems.at[i])
        for i, ((group, place), target) in enumerate(zip(PLACES, targets))
    ]
    for copy in copies:
        copy.start()
    for copy in copies:
        copy.wait()


def delivered(arrived, *after):
    moved = jax.ShapeDtypeStruct((len(PLACES) // 2,) + arrived[0].shape[1:], BF16)
    return pl.pallas_call(
        functools.partial(deliver_kernel, len(arrived)),
        out_shape=(moved, moved),
        in_specs=[ANY] * (len(arrived) + len(after)),
        out_specs=(HBM, HBM),
        scratch_shapes=[pltpu.SemaphoreType.DMA((len(PLACES),))],
        compiler_params=pltpu.CompilerParams(vmem_limit_bytes=4 << 20),
    )(*arrived, *after)


def gate_weights(normed, router_weight, chosen):
    rows, heads, _ = normed.shape
    router = router_weight.reshape(heads, HEAD_DIM, -1)
    logits = jnp.einsum("rhd,hde->re", normed, router, preferred_element_type=F32)
    numbers = jnp.arange(logits.shape[1], dtype=jnp.int32)[None, :]
    first = chosen[:, 0:1]
    second = chosen[:, 1:2]
    first_logit = jnp.sum(jnp.where(numbers == first, logits, 0.0), axis=1, keepdims=True)
    second_logit = jnp.sum(jnp.where(numbers == second, logits, 0.0), axis=1, keepdims=True)
    first_weight = 1.0 / (1.0 + jnp.exp(second_logit - first_logit))
    second_weight = 1.0 / (1.0 + jnp.exp(first_logit - second_logit))
    experts = jnp.arange(EXP_ON, dtype=jnp.int32)[None, :]
    weights = jnp.where(first == experts, first_weight, 0.0) + jnp.where(
        second == experts, second_weight, 0.0
    )
    return weights.T


def body(
    queries,
    residual,
    new_keys,
    new_values,
    key_pool,
    value_pool,
    page_table,
    lengths,
    migrate,
    chosen,
    router_weight,
    w_gate,
    w_up,
    w_down,
):
    length = lax.axis_size("attn")
    swap = length // 2
    masks = list(range(2, swap, 2))
    mine = (lax.axis_index("attn") // (length // EXP_ON)).astype(jnp.int32).reshape(1)
    along = [(i, (i + 1) % length) for i in range(length)]
    plan, keys, values, heads_q, heads_r, *leave = staged(
        page_table, lengths, migrate, chosen, mine, queries, residual, new_keys, new_values,
        key_pool, value_pool,
    )
    arrived = [None] * len(leave)
    arrived[0] = lax.ppermute(leave[0], "attn", along)
    arrived[1] = lax.ppermute(leave[1], "attn", along)
    held = (plan, keys, values, heads_q, heads_r)
    state, normed, own, away = attended(away_kernel, 4, COST, *held)
    swapped = exchanged(away, swap)
    state, normed, own = attended(own_kernel, 3, COST, *held, state, normed, own)
    rows_here = joined(own, swapped, arrived[0])
    others = [exchanged(w, 1) for w in (w_gate, w_up, w_down)]
    blocks = [rows_here] + [exchanged(rows_here, mask) for mask in masks]
    normed, = held_back([normed], rows_here, *others)
    mine_rows = gathered(blocks, normed)
    weights = gate_weights(normed, router_weight, chosen)
    sums = expert_parts(
        mine_rows, [w for pair in zip((w_gate, w_up, w_down), others) for w in pair]
    )
    parts = [sums[i * CAP:(i + 1) * CAP] for i in range(2 * len(blocks))]
    own_parts, away_parts = parts[0::2], parts[1::2]
    back = away_parts[0].astype(F32)
    for part, mask in zip(away_parts[1:][1:] + away_parts[1:][:1], masks[1:] + masks[:1]):
        back = back + exchanged(part, mask).astype(F32)
    own_sums = [own_parts[0]]
    own_sums += [
        exchanged(part, mask)
        for part, mask in zip(own_parts[1:][1:] + own_parts[1:][:1], masks[1:] + masks[:1])
    ]
    away_sums = exchanged(back.astype(BF16), swap)
    moved_keys, moved_values = delivered(arrived, back)
    mixed = finished(plan, mine, weights, state, away_sums, own_sums, in_hbm(moved_keys))
    return (mixed, moved_keys, moved_values)


def solution(mesh):
    placed = (
        P(("groups", "attn"), None),
        P(("groups", "attn"), None),
        P(("groups", "attn"), None),
        P(("groups", "attn"), None),
        P(("groups", "attn"), None, None),
        P(("groups", "attn"), None, None),
        P(("groups", "attn"), None),
        P(("groups", "attn")),
        P(("groups", "attn")),
        P(("groups", "attn"), None),
        P(),
        P(None, "attn"),
        P(None, "attn"),
        P("attn", None),
    )
    return jax.shard_map(
        body,
        mesh=mesh,
        in_specs=placed,
        out_specs=(
            P(("groups", "attn"), None),
            P(("groups", "attn"), None, None),
            P(("groups", "attn"), None, None),
        ),
        check_vma=False,
    )
```

```python
import functools
import math

import jax
import jax.numpy as jnp
from jax import lax
from jax.experimental import pallas as pl
from jax.experimental.pallas import tpu as pltpu
from jax.sharding import PartitionSpec as P

HEAD_DIM = 128
CAP = 5
EXP_ON = 2
F32 = jnp.float32
BF16 = jnp.bfloat16

SMEM = pl.BlockSpec(memory_space=pltpu.SMEM)
VMEM = pl.BlockSpec(memory_space=pltpu.VMEM)
ANY = pl.BlockSpec(memory_space=pl.ANY)
HBM = pl.BlockSpec(memory_space=pltpu.HBM)


def in_hbm(array):
    return pltpu.with_memory_space_constraint(array, pltpu.HBM)


def exchanged(array, mask):
    length = lax.axis_size("attn")
    return lax.ppermute(array, "attn", [(i, i ^ mask) for i in range(length)])


def stage_kernel(table_at, lengths_at, migrate_at, chosen_at, mine, queries_at, residual_at,
                 new_keys_at, new_values_at, key_pool_at, value_pool_at,
                 plan, key_pool, value_pool, heads_q, heads_r, *rest):
    moved, scratch = rest[:len(GROUPS)], rest[len(GROUPS):]
    (table, lengths, migrate, chosen, queries, residual, new_keys, new_values,
     fresh, small_sems, row_sems, pool_sems) = scratch
    pages, rows = table.shape
    page = key_pool.shape[1]
    moves = migrate.shape[0]
    heads = heads_q.shape[0] // rows
    small = [
        pltpu.make_async_copy(source, target, small_sems.at[i])
        for i, (source, target) in enumerate(
            ((table_at, table), (lengths_at, lengths), (migrate_at, migrate), (chosen_at, chosen))
        )
    ]
    wide = [
        pltpu.make_async_copy(source, target, row_sems.at[i])
        for i, (source, target) in enumerate(
            ((queries_at, queries), (residual_at, residual),
             (new_keys_at, new_keys), (new_values_at, new_values))
        )
    ]
    cut = key_pool.shape[0] // POOL_CUTS
    pools = [
        [
            pltpu.make_async_copy(
                source.at[pl.ds(c * cut, cut)], target.at[pl.ds(c * cut, cut)],
                pool_sems.at[side, c],
            )
            for c in range(POOL_CUTS)
        ]
        for side, (source, target) in enumerate(
            ((key_pool_at, key_pool), (value_pool_at, value_pool))
        )
    ]
    for copy in wide[:2] + small + wide[2:] + pools[0] + pools[1]:
        copy.start()
    for copy, target, source in zip(wide[:2], (heads_q, heads_r), (queries, residual)):
        copy.wait()
        for h in range(heads):
            target[pl.ds(h, rows, stride=heads), :] = source[
                :, h * HEAD_DIM:(h + 1) * HEAD_DIM
            ].astype(F32)
    for copy in small:
        copy.wait()
    expert = mine[0]
    other = 1 - expert
    taken_own, taken_away = jnp.int32(0), jnp.int32(0)
    own_slots, away_slots = [], []
    for r in range(rows):
        for p in range(pages):
            plan[p, r] = table[p, r]
        plan[pages, r] = lengths[r]
        first, second = chosen[0, r], chosen[1, r]
        own = ((first == expert) | (second == expert)).astype(jnp.int32)
        away = ((first == other) | (second == other)).astype(jnp.int32)
        own_slots.append(jnp.where(own == 1, taken_own, -1))
        away_slots.append(jnp.where(away == 1, taken_away, -1))
        plan[pages + 1, r] = own_slots[r]
        plan[pages + 2, r] = away_slots[r]
        taken_own = taken_own + own
        taken_away = taken_away + away
    only_own = [
        jnp.where(own_slot >= 0, 1, 0) * jnp.where(away_slot >= 0, 0, 1)
        for own_slot, away_slot in zip(own_slots, away_slots)
    ]
    middle = taken_away
    behind = taken_away + sum(only_own)
    plan[pages + 4, 0] = behind
    for r in range(rows):
        is_away = away_slots[r] >= 0
        is_own = only_own[r] == 1
        place = jnp.where(is_away, away_slots[r], jnp.where(is_own, middle, behind))
        plan[pages + 3, place] = jnp.int32(r)
        middle = middle + only_own[r]
        behind = behind + jnp.where(is_away | is_own, 0, 1)
    for copy, side in zip(wide[2:], (0, 1)):
        copy.wait()
        fresh[side] = (new_keys, new_values)[side][...].astype(F32)
    inside = lax.broadcasted_iota(jnp.int32, (page, key_pool.shape[2]), 0)
    for side, buffer in enumerate((key_pool, value_pool)):
        for copy in pools[side]:
            copy.wait()
        for r in range(rows):
            length = lengths[r]
            last = length // page
            number = table[last, r]
            here = inside == length - last * page
            block = buffer[number].astype(F32)
            buffer[number] = jnp.where(here, fresh[side, r:r + 1, :], block).astype(BF16)
        for m in range(moves):
            request = migrate[m]
            group, place = PLACES[side * moves + m]
            for p in range(pages):
                kept = inside + p * page <= lengths[request]
                block = jnp.where(kept, buffer[table[p, request]].astype(F32), 0.0)
                moved[group][place, p * page:(p + 1) * page, :] = block.astype(BF16)


POOL_CUTS = 3
GROUPS = ((0,), (1, 2, 3))
PLACES = [(g, group.index(i)) for i in range(sum(map(len, GROUPS)))
          for g, group in enumerate(GROUPS) if i in group]
COST = 1 << 20


def staged(page_table, lengths, migrate, chosen, mine, queries, residual, new_keys, new_values,
           key_pool, value_pool):
    rows, width = queries.shape
    heads = width // HEAD_DIM
    kv_width = new_keys.shape[1]
    moves = migrate.shape[0]
    pages = page_table.shape[1]
    moved = tuple(
        jax.ShapeDtypeStruct((len(group), pages * key_pool.shape[1], kv_width), BF16)
        for group in GROUPS
    )
    split = jax.ShapeDtypeStruct((rows * heads, HEAD_DIM), F32)
    return pl.pallas_call(
        stage_kernel,
        out_shape=(
            jax.ShapeDtypeStruct((pages + 5, rows), jnp.int32),
            jax.ShapeDtypeStruct(key_pool.shape, BF16),
            jax.ShapeDtypeStruct(value_pool.shape, BF16),
            split, split,
        ) + moved,
        in_specs=[HBM] * 4 + [SMEM] + [HBM] * 6,
        out_specs=(SMEM,) + (VMEM,) * (4 + len(moved)),
        scratch_shapes=[
            pltpu.SMEM((pages, rows), jnp.int32),
            pltpu.SMEM(lengths.shape, jnp.int32),
            pltpu.SMEM(migrate.shape, jnp.int32),
            pltpu.SMEM((2, rows), jnp.int32),
            pltpu.VMEM(queries.shape, BF16),
            pltpu.VMEM(queries.shape, BF16),
            pltpu.VMEM(new_keys.shape, BF16),
            pltpu.VMEM(new_keys.shape, BF16),
            pltpu.VMEM((2, rows, kv_width), F32),
            pltpu.SemaphoreType.DMA((4,)),
            pltpu.SemaphoreType.DMA((4,)),
            pltpu.SemaphoreType.DMA((2, POOL_CUTS)),
        ],
        compiler_params=pltpu.CompilerParams(vmem_limit_bytes=16 << 20),
        cost_estimate=pl.CostEstimate(flops=0, bytes_accessed=8 << 20, transcendentals=0),
    )(*[in_hbm(a) for a in (page_table.T, lengths, migrate, chosen.T)], mine,
      *[in_hbm(a) for a in (queries, residual, new_keys, new_values, key_pool, value_pool)])


def attend_some(plan, places, key_pool, value_pool, heads_q, heads_r, state_out, normed_out):
    page = key_pool.shape[1]
    kv_heads = key_pool.shape[2] // HEAD_DIM
    rows, heads, _ = state_out.shape
    group = heads // kv_heads
    pages = plan.shape[0] - 5
    positions = pages * page
    head_of = lax.broadcasted_iota(jnp.int32, (heads, HEAD_DIM), 0)
    at_of = lax.broadcasted_iota(jnp.int32, (heads, positions), 1)
    in_group = [(head_of >= g * group) & (head_of < (g + 1) * group) for g in range(kv_heads)]
    some = [plan[pages + 3, place] for place in places]
    starts = [pl.multiple_of(r * heads, 8) for r in some]
    numbers = [[plan[p, r] for p in range(pages)] for r in some]
    queries = [heads_q[pl.ds(start, heads), :] for start in starts]
    spread = [
        jnp.concatenate(
            [jnp.where(inside, query, 0.0).astype(BF16) for inside in in_group], axis=1
        )
        for query in queries
    ]
    scores = [
        lax.dot_general(
            rows_q, jnp.concatenate([key_pool[n] for n in number], axis=0),
            (((1,), (1,)), ((), ())), preferred_element_type=F32,
        ) * (1.0 / math.sqrt(HEAD_DIM))
        for rows_q, number in zip(spread, numbers)
    ]
    visible = [at_of <= plan[pages, r] for r in some]
    scores = [jnp.where(seen, score, -jnp.inf) for seen, score in zip(visible, scores)]
    highest = [jnp.max(score, axis=1, keepdims=True) for score in scores]
    exponent = [
        jnp.where(seen, jnp.exp(score - high), 0.0)
        for seen, score, high in zip(visible, scores, highest)
    ]
    sums = [jnp.sum(e, axis=1, keepdims=True) for e in exponent]
    probs = [(e / s).astype(BF16) for e, s in zip(exponent, sums)]
    mixed = [
        jnp.dot(
            prob, jnp.concatenate([value_pool[n] for n in number], axis=0),
            preferred_element_type=F32,
        )
        for prob, number in zip(probs, numbers)
    ]
    states = []
    for start, mix in zip(starts, mixed):
        attended = mix[:, :HEAD_DIM]
        for g in range(1, kv_heads):
            attended = jnp.where(in_group[g], mix[:, g * HEAD_DIM:(g + 1) * HEAD_DIM], attended)
        states.append(heads_r[pl.ds(start, heads), :] + attended.astype(BF16).astype(F32))
    squares = [
        jnp.sum(jnp.sum(state * state, axis=1, keepdims=True), axis=0, keepdims=True)
        for state in states
    ]
    normed = [
        (state * lax.rsqrt(square / (heads * HEAD_DIM) + 1e-05)).astype(BF16)
        for state, square in zip(states, squares)
    ]
    for r, state, rows_n in zip(some, states, normed):
        state_out[r] = state
        normed_out[r] = rows_n
    return some, normed


def away_kernel(plan, key_pool, value_pool, heads_q, heads_r,
                state_out, normed_out, own_out, away_out):
    pages = plan.shape[0] - 5
    own_out[...] = jnp.zeros_like(own_out)
    away_out[...] = jnp.zeros_like(away_out)
    some, normed = attend_some(
        plan, range(CAP), key_pool, value_pool, heads_q, heads_r, state_out, normed_out
    )
    for r, rows_n in zip(some, normed):
        for row, out in ((pages + 1, own_out), (pages + 2, away_out)):
            slot = plan[row, r]

            @pl.when(slot >= 0)
            def _():
                out[jnp.clip(slot, 0, CAP - 1)] = rows_n


def own_kernel(plan, key_pool, value_pool, heads_q, heads_r, state_in, normed_in, own_in,
               state_out, normed_out, own_out):
    pages = plan.shape[0] - 5
    state_out[...] = state_in[...]
    normed_out[...] = normed_in[...]
    own_out[...] = own_in[...]
    some, normed = attend_some(
        plan, range(CAP, state_out.shape[0]), key_pool, value_pool, heads_q, heads_r, state_out, normed_out
    )
    for r, rows_n in zip(some, normed):
        slot = plan[pages + 1, r]

        @pl.when(slot >= 0)
        def _():
            own_out[jnp.clip(slot, 0, CAP - 1)] = rows_n


def attend_shapes(rows, heads):
    packed = jax.ShapeDtypeStruct((CAP, heads, HEAD_DIM), BF16)
    return (
        jax.ShapeDtypeStruct((rows, heads, HEAD_DIM), F32),
        jax.ShapeDtypeStruct((rows, heads, HEAD_DIM), BF16),
        packed,
        packed,
    )


def attended(kernel, outs, cost, plan, key_pool, value_pool, heads_q, heads_r, *before):
    rows = plan.shape[1]
    heads = heads_q.shape[0] // rows
    return pl.pallas_call(
        kernel,
        out_shape=attend_shapes(rows, heads)[:outs],
        in_specs=[SMEM] + [VMEM] * (4 + len(before)),
        out_specs=(VMEM,) * outs,
        compiler_params=pltpu.CompilerParams(vmem_limit_bytes=8 << 20),
        cost_estimate=pl.CostEstimate(flops=cost, bytes_accessed=cost >> 4, transcendentals=0),
    )(plan, key_pool, value_pool, heads_q, heads_r, *before)


def expert_kernel(block, rows, *rest):
    weights, (sums, split, flat, back) = rest[:6], rest[-4:]
    total, heads, _ = rows.shape
    units = weights[0].shape[1]
    deep = 4 * HEAD_DIM
    wide = 4

    def step(i, carry):
        here = pl.ds(i * block, block)
        split[...] = rows[here].astype(F32).reshape(block * heads, HEAD_DIM)
        for h in range(heads):
            cols = slice(h * HEAD_DIM, (h + 1) * HEAD_DIM)
            flat[:, cols] = split[pl.ds(h, block, stride=heads), :].astype(BF16)
        both = jnp.zeros((block, 4 * units), F32)
        for first in range(0, heads * HEAD_DIM, deep):
            at = slice(first, first + deep)
            both = both + jnp.dot(
                flat[:, at], jnp.concatenate([w[at] for w in weights[:4]], axis=1),
                preferred_element_type=F32,
            )
        gate, up = both[:, :2 * units], both[:, 2 * units:]
        hidden = (gate / (1.0 + jnp.exp(-gate)) * up).astype(BF16)
        for first in range(0, heads, wide):
            cols = slice(first * HEAD_DIM, (first + wide) * HEAD_DIM)
            part = jnp.dot(
                hidden, jnp.concatenate([w[:, cols] for w in weights[4:6]], axis=0),
                preferred_element_type=F32,
            )
            for h in range(wide):
                back[pl.ds(first + h, block, stride=heads), :] = part[
                    :, h * HEAD_DIM:(h + 1) * HEAD_DIM
                ]
        sums[here] = back[...].reshape(block, heads, HEAD_DIM).astype(BF16)
        return carry

    if total == block:
        step(0, 0)
    else:
        lax.fori_loop(0, total // block, step, 0)


def expert_parts(rows, weights, *after):
    total, heads, _ = rows.shape
    block = 8 * CAP
    if total % block:
        block = CAP
    return pl.pallas_call(
        functools.partial(expert_kernel, block),
        out_shape=jax.ShapeDtypeStruct(rows.shape, BF16),
        in_specs=[VMEM] * (1 + len(weights)) + [ANY] * len(after),
        out_specs=VMEM,
        scratch_shapes=[
            pltpu.VMEM((block * heads, HEAD_DIM), F32),
            pltpu.VMEM((block, heads * HEAD_DIM), BF16),
            pltpu.VMEM((block * heads, HEAD_DIM), F32),
        ],
        compiler_params=pltpu.CompilerParams(vmem_limit_bytes=8 << 20),
        cost_estimate=pl.CostEstimate(
            flops=400_000_000, bytes_accessed=10 << 20, transcendentals=10240
        ),
    )(rows, *weights, *after)


def join_kernel(own, away, *rest):
    both = rest[-1]
    both[:CAP] = own[...]
    both[CAP:] = away[...]


def joined(own, away, *after):
    return pl.pallas_call(
        join_kernel,
        out_shape=jax.ShapeDtypeStruct((2 * CAP,) + own.shape[1:], BF16),
        in_specs=[VMEM, VMEM] + [ANY] * len(after),
        out_specs=VMEM,
        compiler_params=pltpu.CompilerParams(vmem_limit_bytes=4 << 20),
    )(own, away, *after)


def hold_kernel(count, *refs):
    for array, copy in zip(refs[:count], refs[-count:]):
        copy[...] = array[...]


def held_back(arrays, *after):
    count = len(arrays)
    return pl.pallas_call(
        functools.partial(hold_kernel, count),
        out_shape=tuple(jax.ShapeDtypeStruct(a.shape, a.dtype) for a in arrays),
        in_specs=[VMEM] * count + [ANY] * len(after),
        out_specs=(VMEM,) * count,
        compiler_params=pltpu.CompilerParams(vmem_limit_bytes=24 << 20),
    )(*arrays, *after)


def gather_kernel(count, *refs):
    blocks, rows = refs[:count], refs[-1]
    size = blocks[0].shape[0]
    for i, block in enumerate(blocks):
        rows[i * size:(i + 1) * size] = block[...]


def gathered(blocks, *after):
    size, heads, depth = blocks[0].shape
    return pl.pallas_call(
        functools.partial(gather_kernel, len(blocks)),
        out_shape=jax.ShapeDtypeStruct((size * len(blocks), heads, depth), BF16),
        in_specs=[VMEM] * len(blocks) + [ANY] * len(after),
        out_specs=VMEM,
        compiler_params=pltpu.CompilerParams(vmem_limit_bytes=24 << 20),
    )(*blocks, *after)


def finish_kernel(count, plan, mine, weights, state, away, *rest):
    owns, rest = rest[:count], rest[count:]
    mixed, rows_split = rest[-2:]
    rows, heads, _ = state.shape
    pages = plan.shape[0] - 5
    expert = mine[0]
    for r in range(rows):
        total = state[r]
        for row, sums, number in ((pages + 1, owns, expert), (pages + 2, (away,), 1 - expert)):
            slot = plan[row, r]
            factor = jnp.where(slot >= 0, weights[number, r], 0.0)
            at = jnp.clip(slot, 0, CAP - 1)
            total = total + factor * sum(part[at].astype(F32) for part in sums)
        rows_split[r * heads:(r + 1) * heads, :] = total
    for h in range(heads):
        mixed[:, h * HEAD_DIM:(h + 1) * HEAD_DIM] = rows_split[
            pl.ds(h, rows, stride=heads), :
        ].astype(BF16)


def finished(plan, mine, weights, state, away, owns, *after):
    rows, heads, _ = state.shape
    return pl.pallas_call(
        functools.partial(finish_kernel, len(owns)),
        out_shape=jax.ShapeDtypeStruct((rows, heads * HEAD_DIM), BF16),
        in_specs=[SMEM] * 3 + [VMEM] * (2 + len(owns)) + [ANY] * len(after),
        out_specs=VMEM,
        scratch_shapes=[pltpu.VMEM((rows * heads, HEAD_DIM), F32)],
        compiler_params=pltpu.CompilerParams(vmem_limit_bytes=8 << 20),
    )(plan, mine, weights, state, away, *owns, *after)


def deliver_kernel(count, *refs):
    arrived, (moved_keys, moved_values, sems) = refs[:count], refs[-3:]
    moves = moved_keys.shape[0]
    targets = [moved.at[m] for moved in (moved_keys, moved_values) for m in range(moves)]
    copies = [
        pltpu.make_async_copy(arrived[group].at[place], target, sems.at[i])
        for i, ((group, place), target) in enumerate(zip(PLACES, targets))
    ]
    for copy in copies:
        copy.start()
    for copy in copies:
        copy.wait()


def delivered(arrived, *after):
    moved = jax.ShapeDtypeStruct((len(PLACES) // 2,) + arrived[0].shape[1:], BF16)
    return pl.pallas_call(
        functools.partial(deliver_kernel, len(arrived)),
        out_shape=(moved, moved),
        in_specs=[ANY] * (len(arrived) + len(after)),
        out_specs=(HBM, HBM),
        scratch_shapes=[pltpu.SemaphoreType.DMA((len(PLACES),))],
        compiler_params=pltpu.CompilerParams(vmem_limit_bytes=4 << 20),
    )(*arrived, *after)


def gate_weights(normed, router_weight, chosen):
    rows, heads, _ = normed.shape
    router = router_weight.reshape(heads, HEAD_DIM, -1)
    logits = jnp.einsum("rhd,hde->re", normed, router, preferred_element_type=F32)
    numbers = jnp.arange(logits.shape[1], dtype=jnp.int32)[None, :]
    first = chosen[:, 0:1]
    second = chosen[:, 1:2]
    first_logit = jnp.sum(jnp.where(numbers == first, logits, 0.0), axis=1, keepdims=True)
    second_logit = jnp.sum(jnp.where(numbers == second, logits, 0.0), axis=1, keepdims=True)
    first_weight = 1.0 / (1.0 + jnp.exp(second_logit - first_logit))
    second_weight = 1.0 / (1.0 + jnp.exp(first_logit - second_logit))
    experts = jnp.arange(EXP_ON, dtype=jnp.int32)[None, :]
    weights = jnp.where(first == experts, first_weight, 0.0) + jnp.where(
        second == experts, second_weight, 0.0
    )
    return weights.T


def body(
    queries,
    residual,
    new_keys,
    new_values,
    key_pool,
    value_pool,
    page_table,
    lengths,
    migrate,
    chosen,
    router_weight,
    w_gate,
    w_up,
    w_down,
):
    length = lax.axis_size("attn")
    swap = length // 2
    masks = list(range(2, swap, 2))
    mine = (lax.axis_index("attn") // (length // EXP_ON)).astype(jnp.int32).reshape(1)
    along = [(i, (i + 1) % length) for i in range(length)]
    plan, keys, values, heads_q, heads_r, *leave = staged(
        page_table, lengths, migrate, chosen, mine, queries, residual, new_keys, new_values,
        key_pool, value_pool,
    )
    arrived = [None] * len(leave)
    arrived[0] = lax.ppermute(leave[0], "attn", along)
    arrived[1] = lax.ppermute(leave[1], "attn", along)
    held = (plan, keys, values, heads_q, heads_r)
    state, normed, own, away = attended(away_kernel, 4, COST, *held)
    swapped = exchanged(away, swap)
    state, normed, own = attended(own_kernel, 3, COST, *held, state, normed, own)
    rows_here = joined(own, swapped, arrived[0])
    others = [exchanged(w, 1) for w in (w_gate, w_up, w_down)]
    blocks = [rows_here] + [exchanged(rows_here, mask) for mask in masks]
    normed, = held_back([normed], rows_here, *others)
    mine_rows = gathered(blocks, normed)
    weights = gate_weights(normed, router_weight, chosen)
    sums = expert_parts(
        mine_rows, [w for pair in zip((w_gate, w_up, w_down), others) for w in pair]
    )
    parts = [sums[i * CAP:(i + 1) * CAP] for i in range(2 * len(blocks))]
    own_parts, away_parts = parts[0::2], parts[1::2]
    back = away_parts[0].astype(F32)
    for part, mask in zip(away_parts[1:][1:] + away_parts[1:][:1], masks[1:] + masks[:1]):
        back = back + exchanged(part, mask).astype(F32)
    own_sums = [own_parts[0]]
    own_sums += [
        exchanged(part, mask)
        for part, mask in zip(own_parts[1:][1:] + own_parts[1:][:1], masks[1:] + masks[:1])
    ]
    away_sums = exchanged(back.astype(BF16), swap)
    moved_keys, moved_values = delivered(arrived, back)
    mixed = finished(plan, mine, weights, state, away_sums, own_sums, in_hbm(moved_keys))
    return (mixed, moved_keys, moved_values)


def solution(mesh):
    placed = (
        P(("groups", "attn"), None),
        P(("groups", "attn"), None),
        P(("groups", "attn"), None),
        P(("groups", "attn"), None),
        P(("groups", "attn"), None, None),
        P(("groups", "attn"), None, None),
        P(("groups", "attn"), None),
        P(("groups", "attn")),
        P(("groups", "attn")),
        P(("groups", "attn"), None),
        P(),
        P(None, "attn"),
        P(None, "attn"),
        P("attn", None),
    )
    return jax.shard_map(
        body,
        mesh=mesh,
        in_specs=placed,
        out_specs=(
            P(("groups", "attn"), None),
            P(("groups", "attn"), None, None),
            P(("groups", "attn"), None, None),
        ),
        check_vma=False,
    )
```
